128 devices in a mesh: rep: 32 (over z, y, x_lo), row: 2 (over core), col: 2 (over x_hi).
Axes of the slice: x: 4 (x_hi: 2, x_lo: 2; x = x_hi * 2 + x_lo), y: 4, z: 4, core: 2. Of those that a mesh axis runs over, the one named last changes fastest.
Arguments:
- fronts: bfloat16 [32, 6144, 6144], P('rep', 'row', 'col'), may hold values from -8 to 72, as said below
- lower_mask: int32 [32, 2, 24], P('rep'), may hold values 0 or 1
- upper_mask: int32 [32, 2, 24], P('rep'), may hold values 0 or 1
Outputs:
- ancestors: float32 [2, 32, 96, 6144], P('row', 'rep', None, 'col')
The draws below stay inside these ranges and needn't reach their ends.
Inputs may be any that keep to these rules, and one draw needn't show every extreme that they name: `fronts`: entries are of order one except on the diagonals of the pivot blocks of g0 and g1, which carry 4 * sqrt(256) more.
All inputs are finite; a program needn't handle non-finite values. No bound on the sum of `lower_mask` or of `upper_mask` on one device may be relied on, other than what follows from the above.
Results may differ from the reference program's by a relative error of at most 0.04.
Values may be sent and summed in bfloat16 or wider, within the bound.
A program may use at most 384 MiB of HBM per device.

```python
import math
import jax
import jax.numpy as jnp
from jax import lax

W = 256
NB = 24
LAYERS = 32
GRID_ROWS = 2
SHARE = 96


def draw_fronts(key, part):
    key = jax.random.fold_in(key, 11)
    full_order = NB * W
    values = jax.random.truncated_normal(key, -6.0, 6.0, (LAYERS, full_order, full_order), jnp.float32)
    places = jnp.arange(full_order, dtype=jnp.int32)
    owners = places // W
    pivots = (owners == 0) | (owners == NB // 2 + 1)
    diagonal = (places[:, None] == places[None, :]) & pivots[:, None]
    values = values + jnp.where(diagonal, jnp.float32(4.0 * math.sqrt(W)), jnp.float32(0.0))[None, :, :]
    return values.astype(jnp.bfloat16)


def plant(values, key, smallest, largest):
    place = [jax.random.randint(jax.random.fold_in(key, axis), (), 0, length) for axis, length in enumerate(values.shape)]
    main_axis = values.shape.index(max(values.shape))
    beside = place[:main_axis] + [(place[main_axis] + 1) % values.shape[main_axis]] + place[main_axis + 1:]
    return values.at[tuple(place)].set(smallest).at[tuple(beside)].set(largest)


def setup_inputs(seed: int = 0) -> dict:
    arg_keys = jax.random.split(jax.random.key(seed), 4)
    fronts = draw_fronts(jax.random.fold_in(arg_keys[3], 71), 0)
    lower_mask = plant((jax.random.randint(arg_keys[1], (LAYERS, 2, NB), 0, 4) < 3).astype(jnp.int32), jax.random.fold_in(arg_keys[1], 1), 0, 1)
    upper_mask = plant((jax.random.randint(arg_keys[2], (LAYERS, 2, NB), 0, 4) < 3).astype(jnp.int32), jax.random.fold_in(arg_keys[2], 1), 0, 1)
    return {"fronts": fronts, "lower_mask": lower_mask, "upper_mask": upper_mask}


def factor(pivot_block):
    size_now = pivot_block.shape[0]
    places = jnp.arange(size_now, dtype=jnp.int32)
    joined = jnp.concatenate([pivot_block, jnp.eye(size_now, dtype=jnp.float32)], axis=1)

    def forward(section, matrix_work):
        pivot_row = lax.dynamic_index_in_dim(matrix_work, section, 0, keepdims=False)
        column = lax.dynamic_index_in_dim(matrix_work, section, 1, keepdims=False)
        pivot_value = lax.dynamic_index_in_dim(column, section, 0, keepdims=False)
        factors = jnp.where(places > section, column / pivot_value, jnp.float32(0.0))
        return matrix_work - factors[:, None] * pivot_row[None, :]

    joined = lax.fori_loop(0, size_now, forward, joined)
    lower_inv = joined[:, size_now:]
    backing = jnp.concatenate([joined[:, :size_now], jnp.eye(size_now, dtype=jnp.float32)], axis=1)

    def backward(turn_index, matrix_work):
        section = size_now - 1 - turn_index
        pivot_row = lax.dynamic_index_in_dim(matrix_work, section, 0, keepdims=False)
        pivot_value = lax.dynamic_index_in_dim(pivot_row, section, 0, keepdims=False)
        scaled = pivot_row / pivot_value
        column = lax.dynamic_index_in_dim(matrix_work, section, 1, keepdims=False)
        factors = jnp.where(places < section, column, jnp.float32(0.0))
        matrix_work = matrix_work - factors[:, None] * scaled[None, :]
        return lax.dynamic_update_index_in_dim(matrix_work, scaled, section, 0)

    backing = lax.fori_loop(0, size_now, backward, backing)
    return lower_inv, backing[:, size_now:]


def panel_pair(column, row_strip, pivot_block, row_keep, col_keep):
    lower_inv, upper_inv = factor(pivot_block)
    lower_part = jnp.dot(column, upper_inv, precision=lax.Precision.HIGHEST, preferred_element_type=jnp.float32)
    upper_part = jnp.dot(lower_inv, row_strip, precision=lax.Precision.HIGHEST, preferred_element_type=jnp.float32)
    return (lower_part * row_keep[:, None]).astype(jnp.bfloat16), (upper_part * col_keep[None, :]).astype(jnp.bfloat16)


def keep_cells(mask_flags, alive_now):
    return jnp.repeat(jnp.where(alive_now, mask_flags, 0).astype(jnp.float32), W)


def reference(fronts, lower_mask, upper_mask):
    first_node = 0
    second_node = NB // 2 + 1
    full_order = NB * W
    blocks = jnp.arange(NB, dtype=jnp.int32)
    alive_one = blocks != first_node
    alive_two = alive_one & (blocks != second_node)
    lo_first, hi_first = first_node * W, first_node * W + W
    lo_second, hi_second = second_node * W, second_node * W + W
    lowers_one, uppers_one, lowers_two, uppers_two = [], [], [], []
    for layer_index in range(LAYERS):
        front_tile = fronts[layer_index]
        column = front_tile[:, lo_first:hi_first].astype(jnp.float32)
        row_strip = front_tile[lo_first:hi_first, :].astype(jnp.float32)
        lower_one, upper_one = panel_pair(column, row_strip, row_strip[:, lo_first:hi_first],
                                          keep_cells(lower_mask[layer_index, 0], alive_one),
                                          keep_cells(upper_mask[layer_index, 0], alive_one))
        column = front_tile[:, lo_second:hi_second].astype(jnp.float32) - jnp.dot(
            lower_one, upper_one[:, lo_second:hi_second], preferred_element_type=jnp.float32)
        row_strip = front_tile[lo_second:hi_second, :].astype(jnp.float32) - jnp.dot(
            lower_one[lo_second:hi_second], upper_one, preferred_element_type=jnp.float32)
        lower_two, upper_two = panel_pair(column, row_strip, row_strip[:, lo_second:hi_second],
                                          keep_cells(lower_mask[layer_index, 1], alive_two),
                                          keep_cells(upper_mask[layer_index, 1], alive_two))
        lowers_one.append(lower_one)
        uppers_one.append(upper_one)
        lowers_two.append(lower_two)
        uppers_two.append(upper_two)
    lowers_one = jnp.stack(lowers_one)
    uppers_one = jnp.stack(uppers_one)
    lowers_two = jnp.stack(lowers_two)
    uppers_two = jnp.stack(uppers_two)
    live_cells = jnp.repeat(alive_two.astype(jnp.float32), W)

    def block_row(block_index):
        row_start = block_index * W
        summed_all = jnp.zeros((W, full_order), jnp.float32)
        for layer_index in range(LAYERS):
            slab_rows = lax.dynamic_slice_in_dim(fronts[layer_index], row_start, W, 0).astype(jnp.float32)
            left_one = lax.dynamic_slice_in_dim(lowers_one[layer_index], row_start, W, 0)
            left_two = lax.dynamic_slice_in_dim(lowers_two[layer_index], row_start, W, 0)
            slab_rows = slab_rows - jnp.dot(left_one, uppers_one[layer_index], preferred_element_type=jnp.float32)
            slab_rows = slab_rows - jnp.dot(left_two, uppers_two[layer_index], preferred_element_type=jnp.float32)
            summed_all = summed_all + slab_rows
        keep_rows = lax.dynamic_slice_in_dim(live_cells, row_start, W, 0)
        return summed_all * keep_rows[:, None] * live_cells[None, :]

    stacked = lax.map(block_row, jnp.arange(NB, dtype=jnp.int32))
    return stacked.reshape(GRID_ROWS, LAYERS, SHARE, full_order)
```

```python
import jax
import jax.numpy as jnp
from jax import lax
from jax.experimental import pallas as pl
from jax.experimental.pallas import tpu as pltpu
from jax.sharding import PartitionSpec as P

W = 256
NB = 24
ROWS = 3072
SHARE = 96
UNIT = 128
BLOCKS = 11
SLOTS = 3
SLABS = 4
STEPS = BLOCKS + 5
MIB = 2**20
MESH = pl.DeviceIdType.MESH
F32 = jnp.float32
BF16 = jnp.bfloat16


def dot(left, right):
    return jnp.dot(left, right, preferred_element_type=F32)


def split(value):
    high = value.astype(BF16)
    return high, (value - high.astype(F32)).astype(BF16)


def place():
    rep, row, col = (lax.axis_index(name) for name in ("rep", "row", "col"))
    return rep // 8, (rep // 2) % 4, rep % 2, row, col


def device(z, y, x, row, col):
    return {"rep": z * 8 + y * 2 + x, "row": row, "col": col}


def gather_kernel(front, corners, strips, send_sem, recv_sem, copy_sem):
    z, y, x, row, col = place()
    beside = device(z, y, x, 1 - row, col)
    across = device(z, y, x, row, 1 - col)
    barrier = pltpu.get_barrier_semaphore()
    for peer in (beside, across):
        pl.semaphore_signal(barrier, inc=1, device_id=peer, device_id_type=MESH)
    pl.semaphore_wait(barrier, 2)
    corner = front.at[pl.ds(row * W, W), pl.ds(col * W, W)]
    strip = front.at[pl.ds(row * W, W), :]

    def remote(src, dst, index, peer):
        return pltpu.make_async_remote_copy(
            src_ref=src, dst_ref=dst, send_sem=send_sem.at[index], recv_sem=recv_sem.at[index],
            device_id=peer, device_id_type=MESH)

    mine = row * 2 + col
    first = remote(corner, corners.at[mine], 0, across)
    first.start()
    second = remote(corner, corners.at[mine], 1, beside)
    second.start()
    third = remote(strip, strips.at[row], 2, beside)
    third.start()
    own_corner = pltpu.make_async_copy(corner, corners.at[mine], copy_sem.at[0])
    own_corner.start()
    own_strip = pltpu.make_async_copy(strip, strips.at[row], copy_sem.at[1])
    own_strip.start()
    first.wait_recv()
    theirs = row * 2 + 1 - col
    fourth = remote(corners.at[theirs], corners.at[theirs], 3, beside)
    fourth.start()
    first.wait_send()
    second.wait()
    third.wait()
    fourth.wait()
    own_corner.wait()
    own_strip.wait()


def invert(pivot, pivot_high, pivot_low, high, low, work):
    rows = lax.broadcasted_iota(jnp.int32, (W, W), 0)
    cols = lax.broadcasted_iota(jnp.int32, (W, W), 1)
    eye = rows == cols
    ones = jnp.where(eye, 1.0, 0.0)
    diag = jnp.where(eye, pivot, 0.0)
    down = jnp.sum(diag, axis=1, keepdims=True)
    along = jnp.sum(diag, axis=0, keepdims=True)
    rest = jnp.where(eye, 0.0, -pivot / along)
    rest_low = rest.astype(BF16)
    guess = (ones + rest) / down
    two = dot(rest_low, rest_low).astype(BF16)
    four = dot(two, two).astype(BF16)
    guess = guess + dot(guess.astype(BF16), two)
    guess = guess + dot(guess.astype(BF16), four)
    guess_high, guess_low = split(guess)
    product = dot(pivot_high, guess_high) + dot(pivot_high, guess_low)
    if pivot_low is not None:
        product = product + dot(pivot_low, guess_high)
    residual = ones - product
    guess = guess + dot(guess_high, residual.astype(BF16))
    size = jnp.max(jnp.sum(jnp.abs(residual), axis=1))
    good = size < 0.03
    work[...] = guess

    @pl.when(jnp.logical_not(good))
    def _():
        work[...] = pivot

        def step(k, carry):
            here = work[...]
            across = work[pl.ds(k, 1), :]
            column = jnp.sum(jnp.where(cols == k, here, 0.0), axis=1, keepdims=True)
            lane = lax.broadcasted_iota(jnp.int32, (1, W), 1) == k
            value = jnp.sum(jnp.where(lane, across, 0.0), axis=1, keepdims=True)
            scaled = jnp.where(lane, 1.0, across) / value
            here = jnp.where(cols == k, 0.0, here) - column * scaled
            work[...] = jnp.where(rows == k, scaled, here)
            return carry

        lax.fori_loop(0, W, step, 0)

    result_high, result_low = split(work[...])
    high[...] = result_high
    low[...] = result_low


def factor_kernel(lower_mask, upper_mask, corners, strips, zero_high, zero_low, one_high, one_low,
                  corner_up, upper, work):
    col = lax.axis_index("col")
    invert(corners[0].astype(F32), corners[0], None, zero_high, zero_low, work)
    keep_low = lower_mask[0, 0, NB // 2 + 1].astype(F32)
    keep_up = upper_mask[0, 0, NB // 2 + 1].astype(F32)
    below = dot(corners[2], zero_high[...]) + dot(corners[2], zero_low[...])
    below = (below * keep_low).astype(BF16)
    right = (corners[1].astype(F32) * keep_up).astype(BF16)
    corner_up[...] = right
    pivot = corners[3].astype(F32) - dot(below, right)
    pivot_high, pivot_low = split(pivot)
    invert(pivot, pivot_high, pivot_low, one_high, one_low, work)
    for block in range(NB // 2):
        span = pl.ds(block * W, W)
        mask_zero = upper_mask[0, 0, col * (NB // 2) + block].astype(F32)
        mask_one = upper_mask[0, 1, col * (NB // 2) + block].astype(F32)
        top = (strips[0, :, span].astype(F32) * mask_zero).astype(BF16)
        upper[0:W, span] = top
        under = strips[1, :, span].astype(F32) - dot(below, top)
        upper[W:2 * W, span] = (under * mask_one).astype(BF16)


def reduce_kernel(lower_mask, front, upper, zero_high, zero_low, one_high, one_low, corner_up, out,
                  panel, lower, slab, snd_one, rcv_one, snd_two, rcv_two, snd_wide, rcv_wide,
                  snd_last, rcv_last, held_one, held_two,
                  panel_sem, slab_sem, snd_one_sem, rcv_one_sem, snd_two_sem, rcv_two_sem,
                  snd_last_sem, rcv_last_sem):
    z, y, x, row, col = place()

    def at_z(k):
        return device((z + k + 4) % 4, y, x, row, col)

    def at_y(k):
        return device(z, (y + k + 4) % 4, x, row, col)

    pair = device(z, y, 1 - x, row, col)
    across = device(z, y, x, row, 1 - col)
    barrier = pltpu.get_barrier_semaphore()
    for peer in (at_z(1), at_z(-1), at_y(1), at_y(-1), pair, across):
        pl.semaphore_signal(barrier, inc=1, device_id=peer, device_id_type=MESH)
    pl.semaphore_wait(barrier, 6)

    order = [(z + k) % 4 for k in (2, 3, 1, 0)]

    def panel_copies(k, quarter):
        source = front.at[quarter, :, :, pl.ds(pl.multiple_of(col * W, W), W)]
        own = pltpu.make_async_copy(source, panel.at[col, quarter], panel_sem.at[0, k])
        remote = pltpu.make_async_remote_copy(
            src_ref=source, dst_ref=panel.at[col, quarter], send_sem=panel_sem.at[1, k],
            recv_sem=panel_sem.at[2, k], device_id=across, device_id_type=MESH)
        return own, remote

    for k in range(4):
        own, remote = panel_copies(k, order[k])
        own.start()
        remote.start()

    def offset(block):
        start = W * (block + 1) - W * col * (1 - jnp.minimum(block, 1))
        return pl.multiple_of(start, W)

    def slab_copy(block):
        return pltpu.make_async_copy(
            front.at[:, :, :, pl.ds(offset(block), W)], slab.at[block % SLABS],
            slab_sem.at[block % SLABS])

    slab_copy(0).start()

    for k in range(4):
        quarter = order[k]
        own, remote = panel_copies(k, quarter)
        own.wait()
        remote.wait()
        left_all = panel[0, quarter].reshape(768, W)
        next_all = panel[1, quarter].reshape(768, W)
        low_zero, low_one = [], []
        for part in range(3):
            span = slice(part * W, part * W + W)
            block = row * (NB // 2) + quarter * 3 + part
            mask_zero = lower_mask[0, 0, block].astype(F32)
            mask_one = lower_mask[0, 1, block].astype(F32)
            first = dot(left_all[span], zero_high[...]) + dot(left_all[span], zero_low[...])
            first = (first * mask_zero).astype(BF16)
            column = next_all[span].astype(F32) - dot(first, corner_up[...])
            column_high, column_low = split(column)
            second = (dot(column_high, one_high[...]) + dot(column_high, one_low[...])
                      + dot(column_low, one_high[...]))
            low_zero.append(first)
            low_one.append((second * mask_one).astype(BF16))
        lower[quarter, :, :, 0:W] = jnp.concatenate(low_zero, axis=0).reshape(4, 192, W)
        lower[quarter, :, :, W:2 * W] = jnp.concatenate(low_one, axis=0).reshape(4, 192, W)

    first_at = (at_z, at_y)
    second_at = (at_y, at_z)
    first_pos = (z, y)
    second_pos = (y, z)

    def way(stream, block):
        turn = 1 - 2 * ((block + stream) % 2)
        return turn

    def product(stream, block, dest):
        span = pl.ds(pl.multiple_of(offset(block) + stream * UNIT, UNIT), UNIT)
        held = block % SLABS
        lanes = slice(stream * UNIT, stream * UNIT + UNIT)
        if stream == 0:
            left = lower[dest]
            here = slab[held, dest, :, :, lanes]
        else:
            left = lower[:, dest]
            here = slab[held, :, dest, :, lanes]
        value = here.reshape(768, UNIT).astype(F32) - dot(left.reshape(768, 2 * W), upper[:, span])
        return value

    def copy_one(stream, kind, block):
        turn = way(stream, block)
        peer = first_at[stream](turn if kind < 2 else -turn)
        return pltpu.make_async_remote_copy(
            src_ref=snd_one.at[stream, kind, block % SLOTS], dst_ref=rcv_one.at[stream, kind, block],
            send_sem=snd_one_sem.at[stream, kind, block % SLOTS],
            recv_sem=rcv_one_sem.at[stream, kind, block], device_id=peer, device_id_type=MESH)

    def send_one(stream, kind, block, value):
        @pl.when(block >= SLOTS)
        def _():
            copy_one(stream, kind, block - SLOTS).wait_send()
        snd_one[stream, kind, block % SLOTS] = value.astype(BF16).reshape(4, 192, UNIT)
        copy_one(stream, kind, block).start()

    def copy_two(stream, kind, block):
        turn = way(stream, block)
        peer = second_at[stream](turn if kind < 2 else -turn)
        if kind == 0:
            src, dst = snd_two.at[stream, block % SLOTS], rcv_two.at[stream, block]
        else:
            src = snd_wide.at[stream, kind - 1, block % SLOTS]
            dst = rcv_wide.at[stream, kind - 1, block]
        return pltpu.make_async_remote_copy(
            src_ref=src, dst_ref=dst, send_sem=snd_two_sem.at[stream, kind, block % SLOTS],
            recv_sem=rcv_two_sem.at[stream, kind, block], device_id=peer, device_id_type=MESH)

    def send_two(stream, kind, block, value):
        @pl.when(block >= SLOTS)
        def _():
            copy_two(stream, kind, block - SLOTS).wait_send()
        if kind == 0:
            snd_two[stream, block % SLOTS] = value.astype(BF16)
        else:
            snd_wide[stream, kind - 1, block % SLOTS] = value
        copy_two(stream, kind, block).start()

    def copy_last(stream, block):
        return pltpu.make_async_remote_copy(
            src_ref=snd_last.at[stream, block % SLOTS], dst_ref=rcv_last.at[stream, block],
            send_sem=snd_last_sem.at[stream, block % SLOTS],
            recv_sem=rcv_last_sem.at[stream, block], device_id=pair, device_id_type=MESH)

    def start_unit(stream, block):
        turn = way(stream, block)
        pos = first_pos[stream]
        send_one(stream, 0, block, product(stream, block, (pos + 2) % 4))
        send_one(stream, 2, block, product(stream, block, (pos - turn + 4) % 4))

    def pass_unit(stream, block):
        turn = way(stream, block)
        pos = first_pos[stream]
        value = product(stream, block, (pos + turn + 4) % 4)
        copy_one(stream, 0, block).wait_recv()
        value = value + rcv_one[stream, 0, block].reshape(768, UNIT).astype(F32)
        send_one(stream, 1, block, value)

    def close_unit(stream, block):
        turn = way(stream, block)
        value = product(stream, block, first_pos[stream])
        copy_one(stream, 2, block).wait_recv()
        value = value + rcv_one[stream, 2, block].reshape(768, UNIT).astype(F32)
        copy_one(stream, 1, block).wait_recv()
        value = value + rcv_one[stream, 1, block].reshape(768, UNIT).astype(F32)
        slot = block % SLABS
        held_one[stream, slot] = value.reshape(4, 192, UNIT)
        pos = second_pos[stream]
        send_two(stream, 0, block, held_one[stream, slot, (pos + 2) % 4])
        send_two(stream, 2, block, held_one[stream, slot, (pos - turn + 4) % 4])

    def pass_sum(stream, block):
        turn = way(stream, block)
        copy_two(stream, 0, block).wait_recv()
        value = held_one[stream, block % SLABS, (second_pos[stream] + turn + 4) % 4]
        send_two(stream, 1, block, value + rcv_two[stream, block].astype(F32))

    def close_sum(stream, block):
        copy_two(stream, 2, block).wait_recv()
        copy_two(stream, 1, block).wait_recv()
        value = held_one[stream, block % SLABS, second_pos[stream]]
        value = value + rcv_wide[stream, 0, block] + rcv_wide[stream, 1, block]
        held_two[stream, block % SLOTS] = value.reshape(2, SHARE, UNIT)

        @pl.when(block >= SLOTS)
        def _():
            copy_last(stream, block - SLOTS).wait_send()
        snd_last[stream, block % SLOTS] = held_two[stream, block % SLOTS, 1 - x]
        copy_last(stream, block).start()

    cells = (z * 8 + y * 2 + x) * SHARE + lax.broadcasted_iota(jnp.int32, (SHARE, UNIT), 0)
    live = (cells < row * W) | (cells >= row * W + W)

    def finish(stream, block):
        copy_last(stream, block).wait_recv()
        value = held_two[stream, block % SLOTS, x] + rcv_last[stream, block]
        span = pl.ds(pl.multiple_of(offset(block) + stream * UNIT, UNIT), UNIT)
        out[:, span] = jnp.where(live, value, 0.0)

    out[:, pl.ds(pl.multiple_of(col * W, W), W)] = jnp.zeros((SHARE, W), F32)

    def when(low, block, function):
        @pl.when((block >= 0) & (block < BLOCKS))
        def _():
            for stream in (0, 1):
                function(stream, block)

    def step(now, carry):
        @pl.when(now < BLOCKS)
        def _():
            slab_copy(now).wait()

        @pl.when(now + 1 < BLOCKS)
        def _():
            slab_copy(now + 1).start()

        when(0, now, start_unit)
        when(1, now - 1, pass_unit)
        when(2, now - 2, close_unit)
        when(3, now - 3, pass_sum)
        when(4, now - 4, close_sum)
        when(5, now - 5, finish)
        return carry

    lax.fori_loop(0, STEPS, step, 0)

    def drain(block, carry):
        for stream in (0, 1):
            for kind in range(3):
                copy_one(stream, kind, block).wait_send()
                copy_two(stream, kind, block).wait_send()
            copy_last(stream, block).wait_send()
        return carry

    lax.fori_loop(BLOCKS - SLOTS, BLOCKS, drain, 0)


def local(fronts, lower_mask, upper_mask):
    any_space = pl.BlockSpec(memory_space=pl.ANY)
    vmem = pl.BlockSpec(memory_space=pltpu.VMEM)
    smem = pl.BlockSpec(memory_space=pltpu.SMEM)
    front = fronts.reshape(ROWS, ROWS)
    corners, strips = pl.pallas_call(
        gather_kernel,
        out_shape=[jax.ShapeDtypeStruct((4, W, W), BF16), jax.ShapeDtypeStruct((2, W, ROWS), BF16)],
        in_specs=[any_space],
        out_specs=[vmem, vmem],
        scratch_shapes=[pltpu.SemaphoreType.DMA((4,)), pltpu.SemaphoreType.DMA((4,)),
                        pltpu.SemaphoreType.DMA((2,))],
        compiler_params=pltpu.CompilerParams(collective_id=0, has_side_effects=True,
                                             vmem_limit_bytes=24 * MIB),
        name="gather_corners",
    )(front)
    block = jax.ShapeDtypeStruct((W, W), BF16)
    factors = pl.pallas_call(
        factor_kernel,
        out_shape=[block] * 5 + [jax.ShapeDtypeStruct((2 * W, ROWS), BF16)],
        in_specs=[smem, smem, vmem, vmem],
        out_specs=[vmem] * 6,
        scratch_shapes=[pltpu.VMEM((W, W), F32)],
        compiler_params=pltpu.CompilerParams(vmem_limit_bytes=32 * MIB),
        name="invert_pivots",
    )(lower_mask, upper_mask, corners, strips)
    zero_high, zero_low, one_high, one_low, corner_up, upper = factors
    dma = pltpu.SemaphoreType.DMA
    out = pl.pallas_call(
        reduce_kernel,
        out_shape=jax.ShapeDtypeStruct((SHARE, ROWS), F32),
        in_specs=[smem, any_space] + [vmem] * 6,
        out_specs=vmem,
        scratch_shapes=[
            pltpu.VMEM((2, 4, 4, 192, W), BF16),
            pltpu.VMEM((4, 4, 192, 2 * W), BF16),
            pltpu.VMEM((SLABS, 4, 4, 192, W), BF16),
            pltpu.VMEM((2, 3, SLOTS, 4, 192, UNIT), BF16),
            pltpu.VMEM((2, 3, BLOCKS, 4, 192, UNIT), BF16),
            pltpu.VMEM((2, SLOTS, 192, UNIT), BF16),
            pltpu.VMEM((2, BLOCKS, 192, UNIT), BF16),
            pltpu.VMEM((2, 2, SLOTS, 192, UNIT), F32),
            pltpu.VMEM((2, 2, BLOCKS, 192, UNIT), F32),
            pltpu.VMEM((2, SLOTS, SHARE, UNIT), F32),
            pltpu.VMEM((2, BLOCKS, SHARE, UNIT), F32),
            pltpu.VMEM((2, SLABS, 4, 192, UNIT), F32),
            pltpu.VMEM((2, SLOTS, 2, SHARE, UNIT), F32),
            dma((3, 4)), dma((SLABS,)), dma((2, 3, SLOTS)), dma((2, 3, BLOCKS)),
            dma((2, 3, SLOTS)), dma((2, 3, BLOCKS)), dma((2, SLOTS)), dma((2, BLOCKS)),
        ],
        compiler_params=pltpu.CompilerParams(collective_id=1, has_side_effects=True,
                                             vmem_limit_bytes=60 * MIB),
        name="reduce_layers",
    )(lower_mask, front.reshape(4, 4, 192, ROWS), upper, zero_high, zero_low, one_high, one_low,
      corner_up)
    return out.reshape(1, 1, SHARE, ROWS)


def solution(mesh):
    in_specs = (P("rep", "row", "col"), P("rep", None, None), P("rep", None, None))
    out_specs = P("row", "rep", None, "col")
    return jax.shard_map(local, mesh=mesh, in_specs=in_specs, out_specs=out_specs, check_vma=False)
```

```python
import jax
import jax.numpy as jnp
from jax import lax
from jax.experimental import pallas as pl
from jax.experimental.pallas import tpu as pltpu
from jax.sharding import PartitionSpec as P

W = 256
NB = 24
ROWS = 3072
SHARE = 96
UNIT = 128
BLOCKS = 11
SLOTS = 3
LAGS = (2, 3, 4, 5)
MIB = 2**20
MESH = pl.DeviceIdType.MESH
F32 = jnp.float32
BF16 = jnp.bfloat16


def dot(left, right):
    return jnp.dot(left, right, preferred_element_type=F32)


def split(value):
    high = value.astype(BF16)
    return high, (value - high.astype(F32)).astype(BF16)


def place():
    rep, row, col = (lax.axis_index(name) for name in ("rep", "row", "col"))
    return rep // 8, (rep // 2) % 4, rep % 2, row, col


def device(z, y, x, row, col):
    return {"rep": z * 8 + y * 2 + x, "row": row, "col": col}


def gather_kernel(front, corners, strip_far, send_sem, recv_sem, copy_sem):
    z, y, x, row, col = place()
    beside = device(z, y, x, 1 - row, col)
    across = device(z, y, x, row, 1 - col)
    barrier = pltpu.get_barrier_semaphore()
    for peer in (beside, across):
        pl.semaphore_signal(barrier, inc=1, device_id=peer, device_id_type=MESH)
    pl.semaphore_wait(barrier, 2)
    corner = front.at[pl.ds(row * W, W), pl.ds(col * W, W)]
    strip = front.at[pl.ds(row * W, W), :]

    def remote(src, dst, index, peer):
        return pltpu.make_async_remote_copy(
            src_ref=src, dst_ref=dst, send_sem=send_sem.at[index], recv_sem=recv_sem.at[index],
            device_id=peer, device_id_type=MESH)

    mine = row * 2 + col
    first = remote(corner, corners.at[mine], 0, across)
    first.start()
    second = remote(corner, corners.at[mine], 1, beside)
    second.start()
    third = remote(strip, strip_far, 2, beside)
    third.start()
    own_corner = pltpu.make_async_copy(corner, corners.at[mine], copy_sem.at[0])
    own_corner.start()
    first.wait_recv()
    theirs = row * 2 + 1 - col
    fourth = remote(corners.at[theirs], corners.at[theirs], 3, beside)
    fourth.start()
    first.wait_send()
    second.wait()
    third.wait()
    fourth.wait()
    own_corner.wait()


def invert(pivot, pivot_high, pivot_low, high, low, work):
    rows = lax.broadcasted_iota(jnp.int32, (W, W), 0)
    cols = lax.broadcasted_iota(jnp.int32, (W, W), 1)
    eye = rows == cols
    ones = jnp.where(eye, 1.0, 0.0)
    diag = jnp.where(eye, pivot, 0.0)
    down = jnp.sum(diag, axis=1, keepdims=True)
    along = jnp.sum(diag, axis=0, keepdims=True)
    rest = jnp.where(eye, 0.0, -pivot / along)
    rest_low = rest.astype(BF16)
    guess = (ones + rest) / down
    two = dot(rest_low, rest_low).astype(BF16)
    four = dot(two, two).astype(BF16)
    guess = guess + dot(guess.astype(BF16), two)
    guess = guess + dot(guess.astype(BF16), four)
    guess_high, guess_low = split(guess)
    product = dot(pivot_high, guess_high) + dot(pivot_high, guess_low)
    if pivot_low is not None:
        product = product + dot(pivot_low, guess_high)
    residual = ones - product
    guess = guess + dot(guess_high, residual.astype(BF16))
    size = jnp.max(jnp.sum(jnp.abs(residual), axis=1))
    good = size < 0.03
    work[...] = guess

    @pl.when(jnp.logical_not(good))
    def _():
        work[...] = pivot

        def step(k, carry):
            here = work[...]
            across = work[pl.ds(k, 1), :]
            column = jnp.sum(jnp.where(cols == k, here, 0.0), axis=1, keepdims=True)
            lane = lax.broadcasted_iota(jnp.int32, (1, W), 1) == k
            value = jnp.sum(jnp.where(lane, across, 0.0), axis=1, keepdims=True)
            scaled = jnp.where(lane, 1.0, across) / value
            here = jnp.where(cols == k, 0.0, here) - column * scaled
            work[...] = jnp.where(rows == k, scaled, here)
            return carry

        lax.fori_loop(0, W, step, 0)

    result_high, result_low = split(work[...])
    high[...] = result_high
    low[...] = result_low


def factor_kernel(lower_mask, upper_mask, front, corners, strip_far, factors, upper_far, work,
                  strips, upper, in_sem, out_sem):
    row, col = lax.axis_index("row"), lax.axis_index("col")

    def strip_copy(part):
        if part == 0:
            source, slot = front.at[pl.ds(pl.multiple_of(row * W, W), W), :], row
        else:
            source, slot = strip_far, 1 - row
        return pltpu.make_async_copy(source, strips.at[slot], in_sem.at[part])

    def upper_copy(block):
        span = pl.ds(block * W, W)
        return pltpu.make_async_copy(upper.at[:, span], upper_far.at[:, span], out_sem.at[block])

    for part in range(2):
        strip_copy(part).start()
    zero_high, zero_low, one_high, one_low = (factors.at[k] for k in range(4))
    invert(corners[0].astype(F32), corners[0], None, zero_high, zero_low, work)
    keep_low = lower_mask[0, 0, NB // 2 + 1].astype(F32)
    keep_up = upper_mask[0, 0, NB // 2 + 1].astype(F32)
    below = dot(corners[2], zero_high[...]) + dot(corners[2], zero_low[...])
    below = (below * keep_low).astype(BF16)
    right = (corners[1].astype(F32) * keep_up).astype(BF16)
    factors[4] = right
    for part in range(2):
        strip_copy(part).wait()
    for block in range(NB // 2):
        span = pl.ds(block * W, W)
        mask_zero = upper_mask[0, 0, col * (NB // 2) + block].astype(F32)
        mask_one = upper_mask[0, 1, col * (NB // 2) + block].astype(F32)
        top = (strips[0, :, span].astype(F32) * mask_zero).astype(BF16)
        upper[0:W, span] = top
        under = strips[1, :, span].astype(F32) - dot(below, top)
        upper[W:2 * W, span] = (under * mask_one).astype(BF16)
        upper_copy(block).start()
    pivot = corners[3].astype(F32) - dot(below, right)
    pivot_high, pivot_low = split(pivot)
    invert(pivot, pivot_high, pivot_low, one_high, one_low, work)
    for block in range(NB // 2):
        upper_copy(block).wait()


def reduce_kernel(lower_mask, front, upper_far, factors, out,
                  upper, lower, tile, snd_first, snd_one, rcv_one, snd_two, rcv_two, snd_wide,
                  rcv_wide, snd_last, rcv_last, held_one, held_two,
                  upper_sem, panel_sem, tile_sem, snd_first_sem, snd_one_sem, rcv_one_sem,
                  snd_two_sem, rcv_two_sem, snd_last_sem, rcv_last_sem):
    z, y, x, row, col = place()

    def at_z(k):
        return device((z + k + 4) % 4, y, x, row, col)

    def at_y(k):
        return device(z, (y + k + 4) % 4, x, row, col)

    first_at = (at_z, at_y)
    second_at = (at_y, at_z)
    first_pos = (z, y)
    second_pos = (y, z)
    pair = device(z, y, 1 - x, row, col)
    across = device(z, y, x, row, 1 - col)
    upper_copy = pltpu.make_async_copy(upper_far, upper, upper_sem.at[0])
    upper_copy.start()

    def offset(block):
        start = W * (block + 1) - W * col * (1 - jnp.minimum(block, 1))
        return pl.multiple_of(start, W)

    def dest_of(stream, kind):
        return (first_pos[stream] + (2, 1, 3, 0)[kind]) % 4

    def tile_copy(stream, kind, i):
        dest, span = dest_of(stream, kind), pl.ds(offset(2 * i + stream), W)
        source = front.at[dest, :, :, span] if stream == 0 else front.at[:, dest, :, span]
        return pltpu.make_async_copy(source, tile.at[stream, kind, i % 2],
                                     tile_sem.at[stream, kind, i % 2])

    for kind in range(4):
        for stream in range(2):
            tile_copy(stream, kind, 0).start()

    barrier = pltpu.get_barrier_semaphore()
    for peer in (at_z(1), at_z(-1), at_y(1), at_y(-1), pair, across):
        pl.semaphore_signal(barrier, inc=1, device_id=peer, device_id_type=MESH)
    pl.semaphore_wait(barrier, 6)

    def piece_copies(dz, dy):
        at, by = (z + dz) % 4, (y + dy) % 4
        span = pl.ds(pl.multiple_of(col * W, W), W)
        source = front.at[at, by, :, span]
        target = lower.at[at, by, :, span]
        own = pltpu.make_async_copy(source, target, panel_sem.at[0, dz, dy])
        remote = pltpu.make_async_remote_copy(
            src_ref=source, dst_ref=target, send_sem=panel_sem.at[1, dz, dy],
            recv_sem=panel_sem.at[2, dz, dy], device_id=across, device_id_type=MESH)
        return own, remote

    def send_piece(dz, dy):
        own, remote = piece_copies(dz, dy)
        own.start()
        remote.start()

    def make_piece(dz, dy):
        own, remote = piece_copies(dz, dy)
        own.wait()
        remote.wait()
        at, by = (z + dz) % 4, (y + dy) % 4
        cell = by * 192 + lax.broadcasted_iota(jnp.int32, (192, W), 0)

        def keep(section):
            first = row * (NB // 2) + at * 3
            flags = [lower_mask[0, section, first + part].astype(F32) for part in range(3)]
            return jnp.where(cell < W, flags[0], jnp.where(cell < 2 * W, flags[1], flags[2]))

        left = lower[at, by, :, 0:W]
        column = lower[at, by, :, W:2 * W].astype(F32)
        first = dot(left, factors[0]) + dot(left, factors[1])
        first = (first * keep(0)).astype(BF16)
        column_high, column_low = split(column - dot(first, factors[4]))
        second = (dot(column_high, factors[2]) + dot(column_high, factors[3])
                  + dot(column_low, factors[2]))
        lower[at, by, :, 0:W] = first
        lower[at, by, :, W:2 * W] = (second * keep(1)).astype(BF16)

    def pieces(count, spot, function):
        def body(k, carry):
            function(*spot(k))
            return carry
        lax.fori_loop(0, count, body, 0)

    groups = (
        (4, lambda k: (2, k)),
        (3, lambda k: ((k + 3) % 4, 2)),
        (9, lambda k: ((1 + 2 * (k // 3) + 3 * (k // 6)) % 4, (k % 3 + 3) % 4)),
    )
    for count, spot in groups:
        pieces(count, spot, send_piece)

    def product(stream, kind, i):
        @pl.when(2 * (i + 1) + stream < BLOCKS)
        def _():
            tile_copy(stream, kind, i + 1).start()
        dest = dest_of(stream, kind)
        left = lower[dest] if stream == 0 else lower[:, dest]
        update = dot(left.reshape(768, 2 * W), upper[:, pl.ds(offset(2 * i + stream), W)])
        tile_copy(stream, kind, i).wait()
        return tile[stream, kind, i % 2].reshape(768, W).astype(F32) - update

    def half_of(value, half):
        return value[:, half * UNIT:half * UNIT + UNIT]

    def peer_of(places_of, half, kind):
        turn = 1 - 2 * half
        return places_of(turn if kind < 2 else -turn)

    def copy_one(stream, kind, half, i):
        if kind == 0:
            src, sem = snd_first.at[half, 2 * i + stream], snd_first_sem.at[half, 2 * i + stream]
        else:
            src = snd_one.at[stream, kind - 1, half, i % SLOTS]
            sem = snd_one_sem.at[stream, kind - 1, half, i % SLOTS]
        return pltpu.make_async_remote_copy(
            src_ref=src, dst_ref=rcv_one.at[kind, half, 2 * i + stream], send_sem=sem,
            recv_sem=rcv_one_sem.at[kind, half, 2 * i + stream],
            device_id=peer_of(first_at[stream], half, kind), device_id_type=MESH)

    def send_one(stream, kind, half, i, value):
        value = value.astype(BF16).reshape(4, 192, UNIT)
        if kind == 0:
            snd_first[half, 2 * i + stream] = value
        else:
            @pl.when(i >= SLOTS)
            def _():
                copy_one(stream, kind, half, i - SLOTS).wait_send()
            snd_one[stream, kind - 1, half, i % SLOTS] = value
        copy_one(stream, kind, half, i).start()

    def got_one(stream, kind, half, i):
        copy_one(stream, kind, half, i).wait_recv()
        return rcv_one[kind, half, 2 * i + stream].reshape(768, UNIT).astype(F32)

    def copy_two(stream, kind, half, i):
        if kind == 0:
            src, dst = snd_two.at[stream, half, i % SLOTS], rcv_two.at[half, 2 * i + stream]
        else:
            src = snd_wide.at[stream, kind - 1, half, i % SLOTS]
            dst = rcv_wide.at[kind - 1, half, 2 * i + stream]
        return pltpu.make_async_remote_copy(
            src_ref=src, dst_ref=dst, send_sem=snd_two_sem.at[stream, kind, half, i % SLOTS],
            recv_sem=rcv_two_sem.at[kind, half, 2 * i + stream],
            device_id=peer_of(second_at[stream], half, kind), device_id_type=MESH)

    def send_two(stream, kind, half, i, value):
        @pl.when(i >= SLOTS)
        def _():
            copy_two(stream, kind, half, i - SLOTS).wait_send()
        if kind == 0:
            snd_two[stream, half, i % SLOTS] = value.astype(BF16)
        else:
            snd_wide[stream, kind - 1, half, i % SLOTS] = value
        copy_two(stream, kind, half, i).start()

    def copy_last(stream, i):
        return pltpu.make_async_remote_copy(
            src_ref=snd_last.at[stream, i % SLOTS], dst_ref=rcv_last.at[2 * i + stream],
            send_sem=snd_last_sem.at[stream, i % SLOTS], recv_sem=rcv_last_sem.at[2 * i + stream],
            device_id=pair, device_id_type=MESH)

    def open_block(stream, i):
        value = product(stream, 0, i)
        for half in range(2):
            send_one(stream, 0, half, i, half_of(value, half))

    def pass_block(stream, i):
        for kind, half in ((1, 0), (2, 1)):
            value = product(stream, kind, i)
            send_one(stream, 2, 1 - half, i, half_of(value, 1 - half))
            send_one(stream, 1, half, i, half_of(value, half) + got_one(stream, 0, half, i))

    def close_block(stream, i):
        value = product(stream, 3, i)
        for half in range(2):
            part = half_of(value, half) + got_one(stream, 2, half, i) + got_one(stream, 1, half, i)
            held_one[stream, i % SLOTS, half] = part.reshape(4, 192, UNIT)
        for half in range(2):
            pos, turn = second_pos[stream], 1 - 2 * half
            send_two(stream, 0, half, i, held_one[stream, i % SLOTS, half, (pos + 2) % 4])
            send_two(stream, 2, half, i, held_one[stream, i % SLOTS, half, (pos - turn + 4) % 4])

    def pass_sum(stream, i):
        for half in range(2):
            pos, turn = second_pos[stream], 1 - 2 * half
            copy_two(stream, 0, half, i).wait_recv()
            value = held_one[stream, i % SLOTS, half, (pos + turn + 4) % 4]
            send_two(stream, 1, half, i, value + rcv_two[half, 2 * i + stream].astype(F32))

    def close_sum(stream, i):
        for half in range(2):
            copy_two(stream, 2, half, i).wait_recv()
            copy_two(stream, 1, half, i).wait_recv()
            value = held_one[stream, i % SLOTS, half, second_pos[stream]]
            value = value + rcv_wide[0, half, 2 * i + stream] + rcv_wide[1, half, 2 * i + stream]
            lanes = slice(half * UNIT, half * UNIT + UNIT)
            held_two[stream, i % SLOTS, :, :, lanes] = value.reshape(2, SHARE, UNIT)

        @pl.when(i >= SLOTS)
        def _():
            copy_last(stream, i - SLOTS).wait_send()
        snd_last[stream, i % SLOTS] = held_two[stream, i % SLOTS, 1 - x]
        copy_last(stream, i).start()

    cells = (z * 8 + y * 2 + x) * SHARE + lax.broadcasted_iota(jnp.int32, (SHARE, W), 0)
    live = (cells < row * W) | (cells >= row * W + W)

    def finish(stream, i):
        copy_last(stream, i).wait_recv()
        value = held_two[stream, i % SLOTS, x] + rcv_last[2 * i + stream]
        out[:, pl.ds(offset(2 * i + stream), W)] = jnp.where(live, value, 0.0)

    counts = ((BLOCKS + 1) // 2, BLOCKS // 2)

    def open_all(stream):
        def body(i, carry):
            open_block(stream, i)
            return carry
        lax.fori_loop(0, counts[stream], body, 0)

    pieces(*groups[0], make_piece)
    upper_copy.wait()
    open_all(0)
    pieces(*groups[1], make_piece)
    open_all(1)
    pieces(*groups[2], make_piece)
    out[:, pl.ds(pl.multiple_of(col * W, W), W)] = jnp.zeros((SHARE, W), F32)

    def when(function, stream, i):
        @pl.when((i >= 0) & (i < counts[stream]))
        def _():
            function(stream, i)

    stages = (pass_block, close_block, pass_sum, close_sum, finish)

    def step(i, carry):
        for half in range(2):
            for stage, lag in zip(stages, (0,) + LAGS):
                stream = (half - lag) % 2
                when(stage, stream, i + (half - lag - stream) // 2)
        return carry

    lax.fori_loop(0, (BLOCKS + LAGS[-1] + 1) // 2, step, 0)

    for stream in range(2):
        def drain_first(i, carry):
            for half in range(2):
                copy_one(stream, 0, half, i).wait_send()
            return carry
        lax.fori_loop(0, counts[stream], drain_first, 0)
        for i in range(counts[stream] - SLOTS, counts[stream]):
            for half in range(2):
                for kind in range(3):
                    if kind:
                        copy_one(stream, kind, half, i).wait_send()
                    copy_two(stream, kind, half, i).wait_send()
            copy_last(stream, i).wait_send()


def local(fronts, lower_mask, upper_mask):
    any_space = pl.BlockSpec(memory_space=pl.ANY)
    vmem = pl.BlockSpec(memory_space=pltpu.VMEM)
    smem = pl.BlockSpec(memory_space=pltpu.SMEM)
    front = fronts.reshape(ROWS, ROWS)
    dma = pltpu.SemaphoreType.DMA
    corners, strip = pl.pallas_call(
        gather_kernel,
        out_shape=[jax.ShapeDtypeStruct((4, W, W), BF16), jax.ShapeDtypeStruct((W, ROWS), BF16)],
        in_specs=[any_space],
        out_specs=[vmem, vmem],
        scratch_shapes=[dma((4,)), dma((4,)), dma((1,))],
        compiler_params=pltpu.CompilerParams(collective_id=0, has_side_effects=True,
                                             vmem_limit_bytes=60 * MIB),
        name="gather_corners",
    )(front)
    factors, upper = pl.pallas_call(
        factor_kernel,
        out_shape=[jax.ShapeDtypeStruct((5, W, W), BF16),
                   jax.ShapeDtypeStruct((2 * W, ROWS), BF16)],
        in_specs=[smem, smem, any_space, vmem, any_space],
        out_specs=[vmem, any_space],
        scratch_shapes=[pltpu.VMEM((W, W), F32), pltpu.VMEM((2, W, ROWS), BF16),
                        pltpu.VMEM((2 * W, ROWS), BF16), dma((2,)), dma((NB // 2,))],
        compiler_params=pltpu.CompilerParams(vmem_limit_bytes=60 * MIB),
        name="invert_pivots",
    )(lower_mask, upper_mask, front, corners, strip)
    out = pl.pallas_call(
        reduce_kernel,
        out_shape=jax.ShapeDtypeStruct((SHARE, ROWS), F32),
        in_specs=[smem, any_space, any_space, vmem],
        out_specs=vmem,
        scratch_shapes=[
            pltpu.VMEM((2 * W, ROWS), BF16),
            pltpu.VMEM((4, 4, 192, 2 * W), BF16),
            pltpu.VMEM((2, 4, 2, 4, 192, W), BF16),
            pltpu.VMEM((2, BLOCKS, 4, 192, UNIT), BF16),
            pltpu.VMEM((2, 2, 2, SLOTS, 4, 192, UNIT), BF16),
            pltpu.VMEM((3, 2, BLOCKS, 4, 192, UNIT), BF16),
            pltpu.VMEM((2, 2, SLOTS, 192, UNIT), BF16),
            pltpu.VMEM((2, BLOCKS, 192, UNIT), BF16),
            pltpu.VMEM((2, 2, 2, SLOTS, 192, UNIT), F32),
            pltpu.VMEM((2, 2, BLOCKS, 192, UNIT), F32),
            pltpu.VMEM((2, SLOTS, SHARE, W), F32),
            pltpu.VMEM((BLOCKS, SHARE, W), F32),
            pltpu.VMEM((2, SLOTS, 2, 4, 192, UNIT), F32),
            pltpu.VMEM((2, SLOTS, 2, SHARE, W), F32),
            dma((1,)), dma((3, 4, 4)), dma((2, 4, 2)), dma((2, BLOCKS)), dma((2, 2, 2, SLOTS)),
            dma((3, 2, BLOCKS)), dma((2, 3, 2, SLOTS)), dma((3, 2, BLOCKS)), dma((2, SLOTS)),
            dma((BLOCKS,)),
        ],
        compiler_params=pltpu.CompilerParams(collective_id=1, has_side_effects=True,
                                             vmem_limit_bytes=60 * MIB),
        name="reduce_layers",
    )(lower_mask, front.reshape(4, 4, 192, ROWS), upper, factors)
    return out.reshape(1, 1, SHARE, ROWS)


def solution(mesh):
    in_specs = (P("rep", "row", "col"), P("rep", None, None), P("rep", None, None))
    out_specs = P("row", "rep", None, "col")
    return jax.shard_map(local, mesh=mesh, in_specs=in_specs, out_specs=out_specs, check_vma=False)
```

```python
import jax
import jax.numpy as jnp
from jax import lax
from jax.experimental import pallas as pl
from jax.experimental.pallas import tpu as pltpu
from jax.sharding import PartitionSpec as P

W = 256
NB = 24
ROWS = 3072
SHARE = 96
UNIT = 128
COUNTS = (5, 4, 1, 1)
BASES = tuple(sum(COUNTS[:k]) for k in range(4))
MAIN = COUNTS[0] + COUNTS[1]
SIDE = COUNTS[2] + COUNTS[3]
SLOTS = 2
SIDE_ORDER = ((3, 0), (2, 0))
LAGS = (2, 3, 4, 5)
SIDE_STEPS = (3, 4)
MIB = 2**20
MESH = pl.DeviceIdType.MESH
F32 = jnp.float32
BF16 = jnp.bfloat16


def dot(left, right):
    return jnp.dot(left, right, preferred_element_type=F32)


def split(value):
    high = value.astype(BF16)
    return high, (value - high.astype(F32)).astype(BF16)


def place():
    rep, row, col = (lax.axis_index(name) for name in ("rep", "row", "col"))
    return rep // 8, (rep // 2) % 4, rep % 2, row, col


def device(z, y, x, row, col):
    return {"rep": z * 8 + y * 2 + x, "row": row, "col": col}


def gather_kernel(front, corners, strip_far, send_sem, recv_sem, copy_sem):
    z, y, x, row, col = place()
    beside = device(z, y, x, 1 - row, col)
    across = device(z, y, x, row, 1 - col)
    barrier = pltpu.get_barrier_semaphore()
    for peer in (beside, across):
        pl.semaphore_signal(barrier, inc=1, device_id=peer, device_id_type=MESH)
    pl.semaphore_wait(barrier, 2)
    corner = front.at[pl.ds(row * W, W), pl.ds(col * W, W)]
    strip = front.at[pl.ds(row * W, W), :]

    def remote(src, dst, index, peer):
        return pltpu.make_async_remote_copy(
            src_ref=src, dst_ref=dst, send_sem=send_sem.at[index], recv_sem=recv_sem.at[index],
            device_id=peer, device_id_type=MESH)

    mine = row * 2 + col
    first = remote(corner, corners.at[mine], 0, across)
    first.start()
    second = remote(corner, corners.at[mine], 1, beside)
    second.start()
    third = remote(strip, strip_far, 2, beside)
    third.start()
    own_corner = pltpu.make_async_copy(corner, corners.at[mine], copy_sem.at[0])
    own_corner.start()
    first.wait_recv()
    theirs = row * 2 + 1 - col
    fourth = remote(corners.at[theirs], corners.at[theirs], 3, beside)
    fourth.start()
    first.wait_send()
    second.wait()
    third.wait()
    fourth.wait()
    own_corner.wait()


def invert(pivot, pivot_high, pivot_low, high, low, work):
    rows = lax.broadcasted_iota(jnp.int32, (W, W), 0)
    cols = lax.broadcasted_iota(jnp.int32, (W, W), 1)
    eye = rows == cols
    ones = jnp.where(eye, 1.0, 0.0)
    diag = jnp.where(eye, pivot, 0.0)
    down = jnp.sum(diag, axis=1, keepdims=True)
    along = jnp.sum(diag, axis=0, keepdims=True)
    rest = jnp.where(eye, 0.0, -pivot / along)
    rest_low = rest.astype(BF16)
    guess = (ones + rest) / down
    two = dot(rest_low, rest_low).astype(BF16)
    four = dot(two, two).astype(BF16)
    guess = guess + dot(guess.astype(BF16), two)
    guess = guess + dot(guess.astype(BF16), four)
    guess_high, guess_low = split(guess)
    product = dot(pivot_high, guess_high) + dot(pivot_high, guess_low)
    if pivot_low is not None:
        product = product + dot(pivot_low, guess_high)
    residual = ones - product
    guess = guess + dot(guess_high, residual.astype(BF16))
    size = jnp.max(jnp.sum(jnp.abs(residual), axis=1))
    good = size < 0.03
    work[...] = guess

    @pl.when(jnp.logical_not(good))
    def _():
        work[...] = pivot

        def step(k, carry):
            here = work[...]
            across = work[pl.ds(k, 1), :]
            column = jnp.sum(jnp.where(cols == k, here, 0.0), axis=1, keepdims=True)
            lane = lax.broadcasted_iota(jnp.int32, (1, W), 1) == k
            value = jnp.sum(jnp.where(lane, across, 0.0), axis=1, keepdims=True)
            scaled = jnp.where(lane, 1.0, across) / value
            here = jnp.where(cols == k, 0.0, here) - column * scaled
            work[...] = jnp.where(rows == k, scaled, here)
            return carry

        lax.fori_loop(0, W, step, 0)

    result_high, result_low = split(work[...])
    high[...] = result_high
    low[...] = result_low


def factor_kernel(lower_mask, upper_mask, front, corners, strip_far, factors, upper_far, work,
                  strips, upper, in_sem, out_sem):
    row, col = lax.axis_index("row"), lax.axis_index("col")

    def strip_copy(part):
        if part == 0:
            source, slot = front.at[pl.ds(pl.multiple_of(row * W, W), W), :], row
        else:
            source, slot = strip_far, 1 - row
        return pltpu.make_async_copy(source, strips.at[slot], in_sem.at[part])

    def upper_copy(block):
        span = pl.ds(block * W, W)
        return pltpu.make_async_copy(upper.at[:, span], upper_far.at[:, span], out_sem.at[block])

    for part in range(2):
        strip_copy(part).start()
    zero_high, zero_low, one_high, one_low = (factors.at[k] for k in range(4))
    invert(corners[0].astype(F32), corners[0], None, zero_high, zero_low, work)
    keep_low = lower_mask[0, 0, NB // 2 + 1].astype(F32)
    keep_up = upper_mask[0, 0, NB // 2 + 1].astype(F32)
    below = dot(corners[2], zero_high[...]) + dot(corners[2], zero_low[...])
    below = (below * keep_low).astype(BF16)
    right = (corners[1].astype(F32) * keep_up).astype(BF16)
    factors[4] = right
    for part in range(2):
        strip_copy(part).wait()
    for block in range(NB // 2):
        span = pl.ds(block * W, W)
        mask_zero = upper_mask[0, 0, col * (NB // 2) + block].astype(F32)
        mask_one = upper_mask[0, 1, col * (NB // 2) + block].astype(F32)
        top = (strips[0, :, span].astype(F32) * mask_zero).astype(BF16)
        upper[0:W, span] = top
        under = strips[1, :, span].astype(F32) - dot(below, top)
        upper[W:2 * W, span] = (under * mask_one).astype(BF16)
        upper_copy(block).start()
    pivot = corners[3].astype(F32) - dot(below, right)
    pivot_high, pivot_low = split(pivot)
    invert(pivot, pivot_high, pivot_low, one_high, one_low, work)
    for block in range(NB // 2):
        upper_copy(block).wait()


class Refs:
    def __init__(self, *refs):
        (self.tile, self.snd_first, self.snd_one, self.rcv_one, self.snd_two, self.rcv_two,
         self.snd_wide, self.rcv_wide, self.held, self.tile_sem, self.first_sem, self.one_snd,
         self.one_rcv, self.two_snd, self.two_rcv) = refs


def reduce_kernel(lower_mask, front, upper_far, factors, out, upper, lower, strip, held_two,
                  snd_last, rcv_last, tile_x, snd_x, rcv_x, upper_sem, panel_sem, strip_sem,
                  last_snd, last_rcv, tile_x_sem, x_snd, x_rcv, *rest):
    main, side = Refs(*rest[:15]), Refs(*rest[15:])
    z, y, x, row, col = place()

    def at_z(k):
        return device((z + k + 4) % 4, y, x, row, col)

    def at_y(k):
        return device(z, (y + k + 4) % 4, x, row, col)

    first_at = (at_z, at_y, at_z, at_y)
    second_at = (at_y, at_z, at_y, at_z)
    first_pos = (z, y, z, y)
    second_pos = (y, z, y, z)
    pair = device(z, y, 1 - x, row, col)
    across = device(z, y, x, row, 1 - col)
    upper_copy = pltpu.make_async_copy(upper_far, upper, upper_sem.at[0])
    upper_copy.start()

    def refs_of(stream):
        return main if stream < 2 else side

    def own(stream, i):
        return BASES[stream] + i - (0 if stream < 2 else MAIN)

    def slot(stream, i):
        return stream * SLOTS + i % SLOTS if stream < 2 else own(stream, i)

    def depth_of(stream):
        return 2 * SHARE if stream < 2 else SHARE

    def span_of(stream, i):
        block = BASES[stream] + i
        start = W * (block + 1) - W * col * (1 - jnp.minimum(block, 1))
        return pl.ds(pl.multiple_of(start, W), W)

    def dest_of(stream, kind):
        return (first_pos[stream] + (2, 1, 3, 0)[kind]) % 4

    def rows_of(ref, stream, kind):
        dest = dest_of(stream, kind)
        return (ref.at[dest], ref.at[:, dest], ref.at[dest, :, x], ref.at[:, dest, x])[stream]

    def tile_copy(stream, kind, i):
        source = rows_of(front, stream, kind)
        source = source.at[(slice(None),) * (3 if stream < 2 else 2) + (span_of(stream, i),)]
        if stream < 2:
            target, sem = main.tile.at[stream, kind - 1, i % 2], main.tile_sem.at[stream, kind - 1, i % 2]
        else:
            target, sem = side.tile.at[own(stream, i), kind], side.tile_sem.at[own(stream, i), kind]
        return pltpu.make_async_copy(source, target, sem)

    def strip_copy(k):
        at, by = opening(k)
        return pltpu.make_async_copy(front.at[(z + at) % 4, (y + by) % 4], strip.at[k % 2],
                                     strip_sem.at[k % 2])

    cross_slot = [SIDE_ORDER.index((stream, i)) % 2 for stream in (2, 3) for i in range(COUNTS[stream])]

    def cross_copy(stream, i):
        source = front.at[:, :, 1 - x, :, span_of(stream, i)]
        index = cross_slot[own(stream, i)]
        return pltpu.make_async_copy(source, tile_x.at[index], tile_x_sem.at[index])

    def opening(k):
        far = ((k + 1) // 2 + 2) % 4
        odd = k % 2
        return odd * 2 + (1 - odd) * far, odd * far + (1 - odd) * 2

    later = (
        (3, lambda k: (1, (1 + 2 * k + 3 * (k // 2)) % 4)),
        (2, lambda k: (3 * (1 - k), 1)),
        (2, lambda k: (3, 3 * (1 - k))),
        (1, lambda k: (0, 3)),
        (1, lambda k: (0, 0)),
    )

    for k in range(2):
        strip_copy(k).start()

    barrier = pltpu.get_barrier_semaphore()
    for peer in (at_z(1), at_z(-1), at_y(1), at_y(-1), pair, across):
        pl.semaphore_signal(barrier, inc=1, device_id=peer, device_id_type=MESH)
    pl.semaphore_wait(barrier, 6)

    def loop(count, function):
        def body(k, carry):
            function(k)
            return carry
        lax.fori_loop(0, count, body, 0)

    def piece_copies(dz, dy):
        at, by = (z + dz) % 4, (y + dy) % 4
        span = pl.ds(pl.multiple_of(col * W, W), W)
        source = front.at[at, by, :, :, span]
        target = lower.at[at, by, :, :, span]
        here = pltpu.make_async_copy(source, target, panel_sem.at[0, dz, dy])
        remote = pltpu.make_async_remote_copy(
            src_ref=source, dst_ref=target, send_sem=panel_sem.at[1, dz, dy],
            recv_sem=panel_sem.at[2, dz, dy], device_id=across, device_id_type=MESH)
        return here, remote

    def send_piece(dz, dy):
        for copy in piece_copies(dz, dy):
            copy.start()

    def make_piece(dz, dy):
        for copy in piece_copies(dz, dy):
            copy.wait()
        at, by = (z + dz) % 4, (y + dy) % 4
        cell = by * 192 + lax.broadcasted_iota(jnp.int32, (192, W), 0)

        def keep(section):
            first = row * (NB // 2) + at * 3
            flags = [lower_mask[0, section, first + part].astype(F32) for part in range(3)]
            return jnp.where(cell < W, flags[0], jnp.where(cell < 2 * W, flags[1], flags[2]))

        left = lower[at, by, :, :, 0:W].reshape(192, W)
        column = lower[at, by, :, :, W:2 * W].reshape(192, W).astype(F32)
        first = dot(left, factors[0]) + dot(left, factors[1])
        first = (first * keep(0)).astype(BF16)
        column_high, column_low = split(column - dot(first, factors[4]))
        second = (dot(column_high, factors[2]) + dot(column_high, factors[3])
                  + dot(column_low, factors[2]))
        second = (second * keep(1)).astype(BF16)
        lower[at, by, :, :, 0:W] = first.reshape(2, SHARE, W)
        lower[at, by, :, :, W:2 * W] = second.reshape(2, SHARE, W)

    loop(7, lambda k: send_piece(*opening(k)))
    for count, spot in later:
        loop(count, lambda k, spot=spot: send_piece(*spot(k)))
    for kind in (1, 2, 3):
        for stream in range(2):
            tile_copy(stream, kind, 0).start()
    for stream, i in SIDE_ORDER[:2]:
        cross_copy(stream, i).start()
    for stream in (2, 3):
        for i in range(COUNTS[stream]):
            for kind in range(4):
                tile_copy(stream, kind, i).start()

    def product(stream, kind, i):
        rows = 4 * depth_of(stream)
        if stream < 2:
            @pl.when(i + 1 < COUNTS[stream])
            def _():
                tile_copy(stream, kind, i + 1).start()
            held = main.tile.at[stream, kind - 1, i % 2]
        else:
            held = side.tile.at[own(stream, i), kind]
        left = rows_of(lower, stream, kind)[...].reshape(rows, 2 * W)
        update = dot(left, upper[:, span_of(stream, i)])
        tile_copy(stream, kind, i).wait()
        value = held[...].reshape(rows, W).astype(F32) - update
        if stream >= 2:
            dest, block = dest_of(stream, kind), own(stream, i)
            other = rcv_x[block, dest] if stream == 2 else rcv_x[block, :, dest]
            value = value + other.reshape(rows, W).astype(F32)
        return value

    def half_of(value, half):
        return value[:, half * UNIT:half * UNIT + UNIT]

    def peer_of(places_of, half, kind):
        turn = 1 - 2 * half
        return places_of(turn if kind < 2 else -turn)

    def copy_one(stream, kind, half, i, part=None):
        refs, block = refs_of(stream), own(stream, i)
        if kind == 0:
            src, sem = refs.snd_first.at[block, half], refs.first_sem.at[block, half]
        else:
            src = refs.snd_one.at[block, kind - 1, half]
            sem = refs.one_snd.at[block, kind - 1, half]
        dst = refs.rcv_one.at[block, kind, half]
        if part is not None:
            src, dst = src.at[part], dst.at[part]
        return pltpu.make_async_remote_copy(
            src_ref=src, dst_ref=dst, send_sem=sem, recv_sem=refs.one_rcv.at[block, kind, half],
            device_id=peer_of(first_at[stream], half, kind), device_id_type=MESH)

    def send_one(stream, kind, half, i, value):
        refs, block = refs_of(stream), own(stream, i)
        value = value.astype(BF16).reshape(4, depth_of(stream), UNIT)
        if kind == 0:
            refs.snd_first[block, half] = value
        else:
            refs.snd_one[block, kind - 1, half] = value
        copy_one(stream, kind, half, i).start()

    def got_one(stream, kind, half, i):
        copy_one(stream, kind, half, i).wait_recv()
        value = refs_of(stream).rcv_one[own(stream, i), kind, half]
        return value.reshape(4 * depth_of(stream), UNIT).astype(F32)

    def copy_two(stream, kind, half, i):
        refs, block, index = refs_of(stream), own(stream, i), slot(stream, i)
        if kind == 0:
            src, dst = refs.snd_two.at[index, half], refs.rcv_two.at[block, half]
        else:
            src = refs.snd_wide.at[index, kind - 1, half]
            dst = refs.rcv_wide.at[block, kind - 1, half]
        return pltpu.make_async_remote_copy(
            src_ref=src, dst_ref=dst, send_sem=refs.two_snd.at[index, kind, half],
            recv_sem=refs.two_rcv.at[block, kind, half],
            device_id=peer_of(second_at[stream], half, kind), device_id_type=MESH)

    def send_two(stream, kind, half, i, value):
        refs, index = refs_of(stream), slot(stream, i)
        if stream < 2:
            @pl.when(i >= SLOTS)
            def _():
                copy_two(stream, kind, half, i - SLOTS).wait_send()
        if kind == 0:
            refs.snd_two[index, half] = value.astype(BF16)
        else:
            refs.snd_wide[index, kind - 1, half] = value
        copy_two(stream, kind, half, i).start()

    def copy_last(stream, i):
        index, block = slot(stream, i), own(stream, i)
        return pltpu.make_async_remote_copy(
            src_ref=snd_last.at[index], dst_ref=rcv_last.at[block], send_sem=last_snd.at[index],
            recv_sem=last_rcv.at[block], device_id=pair, device_id_type=MESH)

    def copy_cross(stream, i):
        block = own(stream, i)
        return pltpu.make_async_remote_copy(
            src_ref=snd_x.at[block], dst_ref=rcv_x.at[block], send_sem=x_snd.at[block],
            recv_sem=x_rcv.at[block], device_id=pair, device_id_type=MESH)

    def open_piece(stream, at, by, k):
        part = by if stream == 0 else at

        def body(i, carry):
            span = span_of(stream, i)
            value = strip[k % 2, :, :, span].reshape(192, W).astype(F32)
            value = value - dot(lower[at, by].reshape(192, 2 * W), upper[:, span])
            for half in range(2):
                main.snd_first[own(stream, i), half, part] = half_of(value, half).astype(BF16)
                copy_one(stream, 0, half, i, part).start()
            return carry
        lax.fori_loop(0, COUNTS[stream], body, 0)

    def open_pieces(k):
        dz, dy = opening(k)
        at, by = (z + dz) % 4, (y + dy) % 4
        make_piece(dz, dy)
        strip_copy(k).wait()

        @pl.when((k == 0) | (k % 2 == 1))
        def _():
            open_piece(0, at, by, k)

        @pl.when(k % 2 == 0)
        def _():
            open_piece(1, at, by, k)

        @pl.when(k + 2 < 7)
        def _():
            strip_copy(k + 2).start()

    def cross_block(stream, i):
        cross_copy(stream, i).wait()
        block = own(stream, i)
        for part in range(2):
            span = pl.ds(2 * part, 2)
            left = lower[span, :, 1 - x].reshape(768, 2 * W)
            value = tile_x[cross_slot[block], span].reshape(768, W).astype(F32)
            value = value - dot(left, upper[:, span_of(stream, i)])
            snd_x[block, span] = value.astype(BF16).reshape(2, 4, SHARE, W)
        copy_cross(stream, i).start()

    def open_block(stream, i):
        copy_cross(stream, i).wait_recv()
        value = product(stream, 0, i)
        for half in range(2):
            send_one(stream, 0, half, i, half_of(value, half))

    def pass_side(stream, ahead, i):
        value = product(stream, 1 + ahead, i)
        send_one(stream, 2, 1 - ahead, i, half_of(value, 1 - ahead))
        send_one(stream, 1, ahead, i, half_of(value, ahead) + got_one(stream, 0, ahead, i))

    def pass_block(stream, i):
        pass_side(stream, 0, i)
        pass_side(stream, 1, i)

    def close_block(stream, i):
        refs, index, depth = refs_of(stream), slot(stream, i), depth_of(stream)
        value = product(stream, 3, i)
        pos = second_pos[stream]
        for half in range(2):
            part = half_of(value, half) + got_one(stream, 2, half, i) + got_one(stream, 1, half, i)
            refs.held[index, half] = part.reshape(4, depth, UNIT)
            send_two(stream, 0, half, i, refs.held[index, half, (pos + 2) % 4])
            send_two(stream, 2, half, i, refs.held[index, half, (pos + 3 + 2 * half) % 4])

    def pass_sum(stream, i):
        refs, index, block = refs_of(stream), slot(stream, i), own(stream, i)
        for half in range(2):
            copy_two(stream, 0, half, i).wait_recv()
            value = refs.held[index, half, (second_pos[stream] + 1 + 2 * half) % 4]
            send_two(stream, 1, half, i, value + refs.rcv_two[block, half].astype(F32))

    def live(width):
        cells = (z * 8 + y * 2 + x) * SHARE + lax.broadcasted_iota(jnp.int32, (SHARE, width), 0)
        return (cells < row * W) | (cells >= row * W + W)

    def close_sum(stream, i):
        refs, index, block = refs_of(stream), slot(stream, i), own(stream, i)
        values = []
        for half in range(2):
            copy_two(stream, 2, half, i).wait_recv()
            copy_two(stream, 1, half, i).wait_recv()
            value = refs.held[index, half, second_pos[stream]]
            values.append(value + refs.rcv_wide[block, 0, half] + refs.rcv_wide[block, 1, half])
        value = jnp.concatenate(values, axis=1)
        if stream >= 2:
            out[:, span_of(stream, i)] = jnp.where(live(W), value, 0.0)
            return
        held_two[index] = value.reshape(2, SHARE, W)

        @pl.when(i >= SLOTS)
        def _():
            copy_last(stream, i - SLOTS).wait_send()
        snd_last[index] = held_two[index, 1 - x]
        copy_last(stream, i).start()

    def finish(stream, i):
        copy_last(stream, i).wait_recv()
        value = held_two[slot(stream, i), x] + rcv_last[own(stream, i)]
        out[:, span_of(stream, i)] = jnp.where(live(W), value, 0.0)

    upper_copy.wait()
    loop(7, open_pieces)
    turns = ((0, 0), (1, 0), (0, 1), (1, 1))
    for k, (count, spot) in enumerate(later):
        loop(count, lambda k, spot=spot: make_piece(*spot(k)))
        if k < len(turns):
            pass_side(*turns[k], 0)
    out[:, pl.ds(pl.multiple_of(col * W, W), W)] = jnp.zeros((SHARE, W), F32)

    def when(function, stream, i):
        @pl.when((i >= 0) & (i < COUNTS[stream]))
        def _():
            function(stream, i)

    def step(now):
        for stream in range(2):
            when(finish, stream, now - LAGS[3])
        for stream in range(2):
            when(close_sum, stream, now - LAGS[2])

        @pl.when(now > 0)
        def _():
            for ahead in range(2):
                for stream in range(2):
                    when(lambda stream, i, ahead=ahead: pass_side(stream, ahead, i), stream, now)
        for k, (stream, i) in enumerate(SIDE_ORDER):
            @pl.when(now == k)
            def _(stream=stream, i=i, k=k):
                cross_block(stream, i)
                if k + 2 < SIDE:
                    cross_copy(*SIDE_ORDER[k + 2]).start()
        for stream in range(2):
            when(pass_sum, stream, now - LAGS[1])
        for stream in range(2):
            when(close_block, stream, now - LAGS[0])
        for k, (stream, i) in enumerate(SIDE_ORDER):
            for shift, stage in enumerate((open_block, pass_block, close_block, pass_sum, close_sum)):
                @pl.when(now == SIDE_STEPS[k] + shift)
                def _(stage=stage, stream=stream, i=i):
                    stage(stream, i)

    loop(max(max(SIDE_STEPS) + 5, max(COUNTS) + LAGS[3]), step)

    for stream in range(4):
        for i in range(COUNTS[stream]):
            for half in range(2):
                for kind in range(3):
                    copy_one(stream, kind, half, i).wait_send()
                    if stream >= 2 or i >= COUNTS[stream] - SLOTS:
                        copy_two(stream, kind, half, i).wait_send()
            if stream >= 2:
                copy_cross(stream, i).wait_send()
            elif i >= COUNTS[stream] - SLOTS:
                copy_last(stream, i).wait_send()


def local(fronts, lower_mask, upper_mask):
    any_space = pl.BlockSpec(memory_space=pl.ANY)
    vmem = pl.BlockSpec(memory_space=pltpu.VMEM)
    smem = pl.BlockSpec(memory_space=pltpu.SMEM)
    front = fronts.reshape(ROWS, ROWS)
    dma = pltpu.SemaphoreType.DMA
    corners, strip = pl.pallas_call(
        gather_kernel,
        out_shape=[jax.ShapeDtypeStruct((4, W, W), BF16), jax.ShapeDtypeStruct((W, ROWS), BF16)],
        in_specs=[any_space],
        out_specs=[vmem, vmem],
        scratch_shapes=[dma((4,)), dma((4,)), dma((1,))],
        compiler_params=pltpu.CompilerParams(collective_id=0, has_side_effects=True,
                                             vmem_limit_bytes=60 * MIB),
        name="gather_corners",
    )(front)
    factors, upper = pl.pallas_call(
        factor_kernel,
        out_shape=[jax.ShapeDtypeStruct((5, W, W), BF16),
                   jax.ShapeDtypeStruct((2 * W, ROWS), BF16)],
        in_specs=[smem, smem, any_space, vmem, any_space],
        out_specs=[vmem, any_space],
        scratch_shapes=[pltpu.VMEM((W, W), F32), pltpu.VMEM((2, W, ROWS), BF16),
                        pltpu.VMEM((2 * W, ROWS), BF16), dma((2,)), dma((NB // 2,))],
        compiler_params=pltpu.CompilerParams(vmem_limit_bytes=60 * MIB),
        name="invert_pivots",
    )(lower_mask, upper_mask, front, corners, strip)
    def group(blocks, slots, depth, tile, rows):
        return [
            pltpu.VMEM(tile + rows + (W,), BF16),
            pltpu.VMEM((blocks, 2, 4, depth, UNIT), BF16),
            pltpu.VMEM((blocks, 2, 2, 4, depth, UNIT), BF16),
            pltpu.VMEM((blocks, 3, 2, 4, depth, UNIT), BF16),
            pltpu.VMEM((slots, 2, depth, UNIT), BF16),
            pltpu.VMEM((blocks, 2, depth, UNIT), BF16),
            pltpu.VMEM((slots, 2, 2, depth, UNIT), F32),
            pltpu.VMEM((blocks, 2, 2, depth, UNIT), F32),
            pltpu.VMEM((slots, 2, 4, depth, UNIT), F32),
            dma(tile), dma((blocks, 2)), dma((blocks, 2, 2)), dma((blocks, 3, 2)),
            dma((slots, 3, 2)), dma((blocks, 3, 2)),
        ]

    main = group(MAIN, 2 * SLOTS, 2 * SHARE, (2, 3, 2), (4, 2, SHARE))
    side = group(SIDE, SIDE, SHARE, (SIDE, 4), (4, SHARE))
    out = pl.pallas_call(
        reduce_kernel,
        out_shape=jax.ShapeDtypeStruct((SHARE, ROWS), F32),
        in_specs=[smem, any_space, any_space, vmem],
        out_specs=vmem,
        scratch_shapes=[
            pltpu.VMEM((2 * W, ROWS), BF16),
            pltpu.VMEM((4, 4, 2, SHARE, 2 * W), BF16),
            pltpu.VMEM((2, 2, SHARE, ROWS), BF16),
            pltpu.VMEM((2 * SLOTS, 2, SHARE, W), F32),
            pltpu.VMEM((2 * SLOTS, SHARE, W), F32),
            pltpu.VMEM((MAIN, SHARE, W), F32),
            pltpu.VMEM((2, 4, 4, SHARE, W), BF16),
            pltpu.VMEM((SIDE, 4, 4, SHARE, W), BF16),
            pltpu.VMEM((SIDE, 4, 4, SHARE, W), BF16),
            dma((1,)), dma((3, 4, 4)), dma((2,)), dma((2 * SLOTS,)), dma((MAIN,)), dma((2,)),
            dma((SIDE,)), dma((SIDE,)),
        ] + main + side,
        compiler_params=pltpu.CompilerParams(collective_id=1, has_side_effects=True,
                                             vmem_limit_bytes=63 * MIB),
        name="reduce_layers",
    )(lower_mask, front.reshape(4, 4, 2, SHARE, ROWS), upper, factors)
    return out.reshape(1, 1, SHARE, ROWS)


def solution(mesh):
    in_specs = (P("rep", "row", "col"), P("rep", None, None), P("rep", None, None))
    out_specs = P("row", "rep", None, "col")
    return jax.shard_map(local, mesh=mesh, in_specs=in_specs, out_specs=out_specs, check_vma=False)
```

```python
import jax
import jax.numpy as jnp
from jax import lax
from jax.experimental import pallas as pl
from jax.experimental.pallas import tpu as pltpu
from jax.sharding import PartitionSpec as P

W = 256
NB = 24
ROWS = 3072
SHARE = 96
UNIT = 128
COUNTS = (5, 4, 1, 1)
BASES = tuple(sum(COUNTS[:k]) for k in range(4))
MAIN = COUNTS[0] + COUNTS[1]
SIDE = COUNTS[2] + COUNTS[3]
SLOTS = 2
SIDE_ORDER = ((3, 0), (2, 0))
LAGS = (2, 3, 4, 5)
SIDE_STEPS = (3, 4)
MIB = 2**20
MESH = pl.DeviceIdType.MESH
F32 = jnp.float32
BF16 = jnp.bfloat16


def dot(left, right):
    return jnp.dot(left, right, preferred_element_type=F32)


def split(value):
    high = value.astype(BF16)
    return high, (value - high.astype(F32)).astype(BF16)


def place():
    rep, row, col = (lax.axis_index(name) for name in ("rep", "row", "col"))
    return rep // 8, (rep // 2) % 4, rep % 2, row, col


def device(z, y, x, row, col):
    return {"rep": z * 8 + y * 2 + x, "row": row, "col": col}


def gather_kernel(front, corners, strip_far, send_sem, recv_sem, copy_sem):
    z, y, x, row, col = place()
    beside = device(z, y, x, 1 - row, col)
    across = device(z, y, x, row, 1 - col)
    barrier = pltpu.get_barrier_semaphore()
    for peer in (beside, across):
        pl.semaphore_signal(barrier, inc=1, device_id=peer, device_id_type=MESH)
    pl.semaphore_wait(barrier, 2)
    corner = front.at[pl.ds(row * W, W), pl.ds(col * W, W)]
    strip = front.at[pl.ds(row * W, W), :]

    def remote(src, dst, index, peer):
        return pltpu.make_async_remote_copy(
            src_ref=src, dst_ref=dst, send_sem=send_sem.at[index], recv_sem=recv_sem.at[index],
            device_id=peer, device_id_type=MESH)

    mine = row * 2 + col
    first = remote(corner, corners.at[mine], 0, across)
    first.start()
    second = remote(corner, corners.at[mine], 1, beside)
    second.start()
    third = remote(strip, strip_far, 2, beside)
    third.start()
    own_corner = pltpu.make_async_copy(corner, corners.at[mine], copy_sem.at[0])
    own_corner.start()
    first.wait_recv()
    theirs = row * 2 + 1 - col
    fourth = remote(corners.at[theirs], corners.at[theirs], 3, beside)
    fourth.start()
    first.wait_send()
    second.wait()
    third.wait()
    fourth.wait()
    own_corner.wait()


def invert(pivot, pivot_high, pivot_low, high, low, work):
    rows = lax.broadcasted_iota(jnp.int32, (W, W), 0)
    cols = lax.broadcasted_iota(jnp.int32, (W, W), 1)
    eye = rows == cols
    ones = jnp.where(eye, 1.0, 0.0)
    diag = jnp.where(eye, pivot, 0.0)
    down = jnp.sum(diag, axis=1, keepdims=True)
    along = jnp.sum(diag, axis=0, keepdims=True)
    rest = jnp.where(eye, 0.0, -pivot / along)
    rest_low = rest.astype(BF16)
    guess = (ones + rest) / down
    two = dot(rest_low, rest_low).astype(BF16)
    four = dot(two, two).astype(BF16)
    guess = guess + dot(guess.astype(BF16), two)
    guess = guess + dot(guess.astype(BF16), four)
    guess_high, guess_low = split(guess)
    product = dot(pivot_high, guess_high) + dot(pivot_high, guess_low)
    if pivot_low is not None:
        product = product + dot(pivot_low, guess_high)
    residual = ones - product
    guess = guess + dot(guess_high, residual.astype(BF16))
    size = jnp.max(jnp.sum(jnp.abs(residual), axis=1))
    good = size < 0.03
    work[...] = guess

    @pl.when(jnp.logical_not(good))
    def _():
        work[...] = pivot

        def step(k, carry):
            here = work[...]
            across = work[pl.ds(k, 1), :]
            column = jnp.sum(jnp.where(cols == k, here, 0.0), axis=1, keepdims=True)
            lane = lax.broadcasted_iota(jnp.int32, (1, W), 1) == k
            value = jnp.sum(jnp.where(lane, across, 0.0), axis=1, keepdims=True)
            scaled = jnp.where(lane, 1.0, across) / value
            here = jnp.where(cols == k, 0.0, here) - column * scaled
            work[...] = jnp.where(rows == k, scaled, here)
            return carry

        lax.fori_loop(0, W, step, 0)

    result_high, result_low = split(work[...])
    high[...] = result_high
    low[...] = result_low


def factor_kernel(lower_mask, upper_mask, front, corners, strip_far, factors, upper_far, work,
                  strips, upper, in_sem, out_sem):
    row, col = lax.axis_index("row"), lax.axis_index("col")

    def strip_copy(part):
        if part == 0:
            source, slot = front.at[pl.ds(pl.multiple_of(row * W, W), W), :], row
        else:
            source, slot = strip_far, 1 - row
        return pltpu.make_async_copy(source, strips.at[slot], in_sem.at[part])

    def upper_copy(block):
        span = pl.ds(block * W, W)
        return pltpu.make_async_copy(upper.at[:, span], upper_far.at[:, span], out_sem.at[block])

    for part in range(2):
        strip_copy(part).start()
    zero_high, zero_low, one_high, one_low = (factors.at[k] for k in range(4))
    invert(corners[0].astype(F32), corners[0], None, zero_high, zero_low, work)
    keep_low = lower_mask[0, 0, NB // 2 + 1].astype(F32)
    keep_up = upper_mask[0, 0, NB // 2 + 1].astype(F32)
    below = dot(corners[2], zero_high[...]) + dot(corners[2], zero_low[...])
    below = (below * keep_low).astype(BF16)
    right = (corners[1].astype(F32) * keep_up).astype(BF16)
    factors[4] = right
    for part in range(2):
        strip_copy(part).wait()
    for block in range(NB // 2):
        span = pl.ds(block * W, W)
        mask_zero = upper_mask[0, 0, col * (NB // 2) + block].astype(F32)
        mask_one = upper_mask[0, 1, col * (NB // 2) + block].astype(F32)
        top = (strips[0, :, span].astype(F32) * mask_zero).astype(BF16)
        upper[0:W, span] = top
        under = strips[1, :, span].astype(F32) - dot(below, top)
        upper[W:2 * W, span] = (under * mask_one).astype(BF16)
        upper_copy(block).start()
    pivot = corners[3].astype(F32) - dot(below, right)
    pivot_high, pivot_low = split(pivot)
    invert(pivot, pivot_high, pivot_low, one_high, one_low, work)
    for block in range(NB // 2):
        upper_copy(block).wait()


class Refs:
    def __init__(self, *refs):
        (self.tile, self.snd_first, self.snd_one, self.rcv_one, self.snd_two, self.rcv_two,
         self.snd_wide, self.rcv_wide, self.held, self.tile_sem, self.first_sem, self.one_snd,
         self.one_rcv, self.two_snd, self.two_rcv) = refs


def reduce_kernel(lower_mask, front, upper_far, factors, out, upper, lower, strip, held_two,
                  snd_last, rcv_last, tile_x, snd_x, rcv_x, upper_sem, panel_sem, strip_sem,
                  last_snd, last_rcv, tile_x_sem, x_snd, x_rcv, *rest):
    main, side = Refs(*rest[:15]), Refs(*rest[15:])
    z, y, x, row, col = place()

    def at_z(k):
        return device((z + k + 4) % 4, y, x, row, col)

    def at_y(k):
        return device(z, (y + k + 4) % 4, x, row, col)

    first_at = (at_z, at_y, at_z, at_y)
    second_at = (at_y, at_z, at_y, at_z)
    first_pos = (z, y, z, y)
    second_pos = (y, z, y, z)
    pair = device(z, y, 1 - x, row, col)
    across = device(z, y, x, row, 1 - col)
    upper_copy = pltpu.make_async_copy(upper_far, upper, upper_sem.at[0])
    upper_copy.start()

    def refs_of(stream):
        return main if stream < 2 else side

    def own(stream, i):
        return BASES[stream] + i - (0 if stream < 2 else MAIN)

    def slot(stream, i):
        return stream * SLOTS + i % SLOTS if stream < 2 else own(stream, i)

    def depth_of(stream):
        return 2 * SHARE if stream < 2 else SHARE

    def span_of(stream, i):
        block = BASES[stream] + i
        start = W * (block + 1) - W * col * (1 - jnp.minimum(block, 1))
        return pl.ds(pl.multiple_of(start, W), W)

    def dest_of(stream, kind):
        return (first_pos[stream] + (2, 1, 3, 0)[kind]) % 4

    def rows_of(ref, stream, kind):
        dest = dest_of(stream, kind)
        return (ref.at[dest], ref.at[:, dest], ref.at[dest, :, x], ref.at[:, dest, x])[stream]

    def tile_copy(stream, kind, i):
        source = rows_of(front, stream, kind)
        source = source.at[(slice(None),) * (3 if stream < 2 else 2) + (span_of(stream, i),)]
        if stream < 2:
            target, sem = main.tile.at[stream, kind - 1, i % 2], main.tile_sem.at[stream, kind - 1, i % 2]
        else:
            target, sem = side.tile.at[own(stream, i), kind], side.tile_sem.at[own(stream, i), kind]
        return pltpu.make_async_copy(source, target, sem)

    def strip_copy(k):
        at, by = opening(k)
        return pltpu.make_async_copy(front.at[(z + at) % 4, (y + by) % 4], strip.at[k % 2],
                                     strip_sem.at[k % 2])

    cross_slot = [SIDE_ORDER.index((stream, i)) % 2 for stream in (2, 3) for i in range(COUNTS[stream])]

    def cross_copy(stream, i):
        source = front.at[:, :, 1 - x, :, span_of(stream, i)]
        index = cross_slot[own(stream, i)]
        return pltpu.make_async_copy(source, tile_x.at[index], tile_x_sem.at[index])

    def opening(k):
        far = ((k + 1) // 2 + 2) % 4
        odd = k % 2
        return odd * 2 + (1 - odd) * far, odd * far + (1 - odd) * 2

    later = (
        (3, lambda k: (1, (1 + 2 * k + 3 * (k // 2)) % 4)),
        (2, lambda k: (3 * (1 - k), 1)),
        (2, lambda k: (3, 3 * (1 - k))),
        (1, lambda k: (0, 3)),
        (1, lambda k: (0, 0)),
    )

    for k in range(2):
        strip_copy(k).start()

    barrier = pltpu.get_barrier_semaphore()
    for peer in (at_z(1), at_z(-1), at_y(1), at_y(-1), pair, across):
        pl.semaphore_signal(barrier, inc=1, device_id=peer, device_id_type=MESH)
    pl.semaphore_wait(barrier, 6)

    def loop(count, function):
        def body(k, carry):
            function(k)
            return carry
        lax.fori_loop(0, count, body, 0)

    def piece_copies(dz, dy):
        at, by = (z + dz) % 4, (y + dy) % 4
        span = pl.ds(pl.multiple_of(col * W, W), W)
        source = front.at[at, by, :, :, span]
        target = lower.at[at, by, :, :, span]
        here = pltpu.make_async_copy(source, target, panel_sem.at[0, dz, dy])
        remote = pltpu.make_async_remote_copy(
            src_ref=source, dst_ref=target, send_sem=panel_sem.at[1, dz, dy],
            recv_sem=panel_sem.at[2, dz, dy], device_id=across, device_id_type=MESH)
        return here, remote

    def send_piece(dz, dy):
        for copy in piece_copies(dz, dy):
            copy.start()

    def make_piece(dz, dy):
        for copy in piece_copies(dz, dy):
            copy.wait()
        at, by = (z + dz) % 4, (y + dy) % 4
        cell = by * 192 + lax.broadcasted_iota(jnp.int32, (192, W), 0)

        def keep(section):
            first = row * (NB // 2) + at * 3
            flags = [lower_mask[0, section, first + part].astype(F32) for part in range(3)]
            return jnp.where(cell < W, flags[0], jnp.where(cell < 2 * W, flags[1], flags[2]))

        left = lower[at, by, :, :, 0:W].reshape(192, W)
        column = lower[at, by, :, :, W:2 * W].reshape(192, W).astype(F32)
        first = dot(left, factors[0]) + dot(left, factors[1])
        first = (first * keep(0)).astype(BF16)
        column_high, column_low = split(column - dot(first, factors[4]))
        second = (dot(column_high, factors[2]) + dot(column_high, factors[3])
                  + dot(column_low, factors[2]))
        second = (second * keep(1)).astype(BF16)
        lower[at, by, :, :, 0:W] = first.reshape(2, SHARE, W)
        lower[at, by, :, :, W:2 * W] = second.reshape(2, SHARE, W)

    loop(7, lambda k: send_piece(*opening(k)))
    for count, spot in later:
        loop(count, lambda k, spot=spot: send_piece(*spot(k)))
    for kind in (1, 2, 3):
        for stream in range(2):
            tile_copy(stream, kind, 0).start()
    for stream, i in SIDE_ORDER[:2]:
        cross_copy(stream, i).start()
    for stream in (2, 3):
        for i in range(COUNTS[stream]):
            for kind in range(4):
                tile_copy(stream, kind, i).start()

    def product(stream, kind, i):
        rows = 4 * depth_of(stream)
        if stream < 2:
            @pl.when(i + 1 < COUNTS[stream])
            def _():
                tile_copy(stream, kind, i + 1).start()
            held = main.tile.at[stream, kind - 1, i % 2]
        else:
            held = side.tile.at[own(stream, i), kind]
        left = rows_of(lower, stream, kind)[...].reshape(rows, 2 * W)
        update = dot(left, upper[:, span_of(stream, i)])
        tile_copy(stream, kind, i).wait()
        value = held[...].reshape(rows, W).astype(F32) - update
        if stream >= 2:
            dest, block = dest_of(stream, kind), own(stream, i)
            other = rcv_x[block, dest] if stream == 2 else rcv_x[block, :, dest]
            value = value + other.reshape(rows, W).astype(F32)
        return value

    def half_of(value, half):
        return value[:, half * UNIT:half * UNIT + UNIT]

    def peer_of(places_of, half, kind):
        turn = 1 - 2 * half
        return places_of(turn if kind < 2 else -turn)

    def copy_one(stream, kind, half, i, part=None):
        refs, block = refs_of(stream), own(stream, i)
        if kind == 0:
            src, sem = refs.snd_first.at[block, half], refs.first_sem.at[block, half]
        else:
            src = refs.snd_one.at[block, kind - 1, half]
            sem = refs.one_snd.at[block, kind - 1, half]
        dst = refs.rcv_one.at[block, kind, half]
        if part is not None:
            src, dst = src.at[part], dst.at[part]
        return pltpu.make_async_remote_copy(
            src_ref=src, dst_ref=dst, send_sem=sem, recv_sem=refs.one_rcv.at[block, kind, half],
            device_id=peer_of(first_at[stream], half, kind), device_id_type=MESH)

    def send_one(stream, kind, half, i, value):
        refs, block = refs_of(stream), own(stream, i)
        value = value.astype(BF16).reshape(4, depth_of(stream), UNIT)
        if kind == 0:
            refs.snd_first[block, half] = value
        else:
            refs.snd_one[block, kind - 1, half] = value
        copy_one(stream, kind, half, i).start()

    def got_one(stream, kind, half, i):
        copy_one(stream, kind, half, i).wait_recv()
        value = refs_of(stream).rcv_one[own(stream, i), kind, half]
        return value.reshape(4 * depth_of(stream), UNIT).astype(F32)

    def copy_two(stream, kind, half, i):
        refs, block, index = refs_of(stream), own(stream, i), slot(stream, i)
        if kind == 0:
            src, dst = refs.snd_two.at[index, half], refs.rcv_two.at[block, half]
        else:
            src = refs.snd_wide.at[index, kind - 1, half]
            dst = refs.rcv_wide.at[block, kind - 1, half]
        return pltpu.make_async_remote_copy(
            src_ref=src, dst_ref=dst, send_sem=refs.two_snd.at[index, kind, half],
            recv_sem=refs.two_rcv.at[block, kind, half],
            device_id=peer_of(second_at[stream], half, kind), device_id_type=MESH)

    def send_two(stream, kind, half, i, value):
        refs, index = refs_of(stream), slot(stream, i)
        if stream < 2:
            @pl.when(i >= SLOTS)
            def _():
                copy_two(stream, kind, half, i - SLOTS).wait_send()
        if kind == 0:
            refs.snd_two[index, half] = value.astype(BF16)
        else:
            refs.snd_wide[index, kind - 1, half] = value
        copy_two(stream, kind, half, i).start()

    def copy_last(stream, i):
        index, block = slot(stream, i), own(stream, i)
        return pltpu.make_async_remote_copy(
            src_ref=snd_last.at[index], dst_ref=rcv_last.at[block], send_sem=last_snd.at[index],
            recv_sem=last_rcv.at[block], device_id=pair, device_id_type=MESH)

    def copy_cross(stream, i):
        block = own(stream, i)
        return pltpu.make_async_remote_copy(
            src_ref=snd_x.at[block], dst_ref=rcv_x.at[block], send_sem=x_snd.at[block],
            recv_sem=x_rcv.at[block], device_id=pair, device_id_type=MESH)

    def open_piece(stream, at, by, k):
        part = by if stream == 0 else at

        def body(i, carry):
            span = span_of(stream, i)
            value = strip[k % 2, :, :, span].reshape(192, W).astype(F32)
            value = value - dot(lower[at, by].reshape(192, 2 * W), upper[:, span])
            for half in range(2):
                main.snd_first[own(stream, i), half, part] = half_of(value, half).astype(BF16)
                copy_one(stream, 0, half, i, part).start()
            return carry
        lax.fori_loop(0, COUNTS[stream], body, 0)

    def open_pieces(k):
        dz, dy = opening(k)
        at, by = (z + dz) % 4, (y + dy) % 4
        make_piece(dz, dy)
        strip_copy(k).wait()

        @pl.when((k == 0) | (k % 2 == 1))
        def _():
            open_piece(0, at, by, k)

        @pl.when(k % 2 == 0)
        def _():
            open_piece(1, at, by, k)

        @pl.when(k + 2 < 7)
        def _():
            strip_copy(k + 2).start()

    def cross_block(stream, i):
        cross_copy(stream, i).wait()
        block = own(stream, i)
        for part in range(2):
            span = pl.ds(2 * part, 2)
            left = lower[span, :, 1 - x].reshape(768, 2 * W)
            value = tile_x[cross_slot[block], span].reshape(768, W).astype(F32)
            value = value - dot(left, upper[:, span_of(stream, i)])
            snd_x[block, span] = value.astype(BF16).reshape(2, 4, SHARE, W)
        copy_cross(stream, i).start()

    def open_block(stream, i):
        copy_cross(stream, i).wait_recv()
        value = product(stream, 0, i)
        for half in range(2):
            send_one(stream, 0, half, i, half_of(value, half))

    def pass_side(stream, ahead, i):
        value = product(stream, 1 + ahead, i)
        send_one(stream, 2, 1 - ahead, i, half_of(value, 1 - ahead))
        send_one(stream, 1, ahead, i, half_of(value, ahead) + got_one(stream, 0, ahead, i))

    def pass_block(stream, i):
        pass_side(stream, 0, i)
        pass_side(stream, 1, i)

    def close_block(stream, i):
        refs, index, depth = refs_of(stream), slot(stream, i), depth_of(stream)
        value = product(stream, 3, i)
        pos = second_pos[stream]
        for half in range(2):
            part = half_of(value, half) + got_one(stream, 2, half, i) + got_one(stream, 1, half, i)
            refs.held[index, half] = part.reshape(4, depth, UNIT)
            send_two(stream, 0, half, i, refs.held[index, half, (pos + 2) % 4])
            send_two(stream, 2, half, i, refs.held[index, half, (pos + 3 + 2 * half) % 4])

    def pass_sum(stream, i):
        refs, index, block = refs_of(stream), slot(stream, i), own(stream, i)
        for half in range(2):
            copy_two(stream, 0, half, i).wait_recv()
            value = refs.held[index, half, (second_pos[stream] + 1 + 2 * half) % 4]
            send_two(stream, 1, half, i, value + refs.rcv_two[block, half].astype(F32))

    def live(width):
        cells = (z * 8 + y * 2 + x) * SHARE + lax.broadcasted_iota(jnp.int32, (SHARE, width), 0)
        return (cells < row * W) | (cells >= row * W + W)

    def close_sum(stream, i):
        refs, index, block = refs_of(stream), slot(stream, i), own(stream, i)
        values = []
        for half in range(2):
            copy_two(stream, 2, half, i).wait_recv()
            copy_two(stream, 1, half, i).wait_recv()
            value = refs.held[index, half, second_pos[stream]]
            values.append(value + refs.rcv_wide[block, 0, half] + refs.rcv_wide[block, 1, half])
        value = jnp.concatenate(values, axis=1)
        if stream >= 2:
            out[:, span_of(stream, i)] = jnp.where(live(W), value, 0.0)
            return
        held_two[index] = value.reshape(2, SHARE, W)

        @pl.when(i >= SLOTS)
        def _():
            copy_last(stream, i - SLOTS).wait_send()
        snd_last[index] = held_two[index, 1 - x]
        copy_last(stream, i).start()

    def finish(stream, i):
        copy_last(stream, i).wait_recv()
        value = held_two[slot(stream, i), x] + rcv_last[own(stream, i)]
        out[:, span_of(stream, i)] = jnp.where(live(W), value, 0.0)

    upper_copy.wait()
    loop(7, open_pieces)
    turns = ((0, 0), (1, 0), (0, 1), (1, 1))
    for k, (count, spot) in enumerate(later):
        loop(count, lambda k, spot=spot: make_piece(*spot(k)))
        if k < len(turns):
            pass_side(*turns[k], 0)
    out[:, pl.ds(pl.multiple_of(col * W, W), W)] = jnp.zeros((SHARE, W), F32)

    def when(function, stream, i):
        @pl.when((i >= 0) & (i < COUNTS[stream]))
        def _():
            function(stream, i)

    def step(now):

        @pl.when(now > 0)
        def _():
            for ahead in range(2):
                for stream in range(2):
                    when(lambda stream, i, ahead=ahead: pass_side(stream, ahead, i), stream, now)
        for k, (stream, i) in enumerate(SIDE_ORDER):
            @pl.when(now == k)
            def _(stream=stream, i=i, k=k):
                cross_block(stream, i)
                if k + 2 < SIDE:
                    cross_copy(*SIDE_ORDER[k + 2]).start()
        for stream in range(2):
            when(finish, stream, now - LAGS[3])
        for stream in range(2):
            when(close_sum, stream, now - LAGS[2])
        for stream in range(2):
            when(pass_sum, stream, now - LAGS[1])
        for stream in range(2):
            when(close_block, stream, now - LAGS[0])
        for k, (stream, i) in enumerate(SIDE_ORDER):
            for shift, stage in enumerate((open_block, pass_block, close_block, pass_sum, close_sum)):
                @pl.when(now == SIDE_STEPS[k] + shift)
                def _(stage=stage, stream=stream, i=i):
                    stage(stream, i)

    loop(max(max(SIDE_STEPS) + 5, max(COUNTS) + LAGS[3]), step)

    for stream in range(4):
        for i in range(COUNTS[stream]):
            for half in range(2):
                for kind in range(3):
                    copy_one(stream, kind, half, i).wait_send()
                    if stream >= 2 or i >= COUNTS[stream] - SLOTS:
                        copy_two(stream, kind, half, i).wait_send()
            if stream >= 2:
                copy_cross(stream, i).wait_send()
            elif i >= COUNTS[stream] - SLOTS:
                copy_last(stream, i).wait_send()


def local(fronts, lower_mask, upper_mask):
    any_space = pl.BlockSpec(memory_space=pl.ANY)
    vmem = pl.BlockSpec(memory_space=pltpu.VMEM)
    smem = pl.BlockSpec(memory_space=pltpu.SMEM)
    front = fronts.reshape(ROWS, ROWS)
    dma = pltpu.SemaphoreType.DMA
    corners, strip = pl.pallas_call(
        gather_kernel,
        out_shape=[jax.ShapeDtypeStruct((4, W, W), BF16), jax.ShapeDtypeStruct((W, ROWS), BF16)],
        in_specs=[any_space],
        out_specs=[vmem, vmem],
        scratch_shapes=[dma((4,)), dma((4,)), dma((1,))],
        compiler_params=pltpu.CompilerParams(collective_id=0, has_side_effects=True,
                                             vmem_limit_bytes=60 * MIB),
        name="gather_corners",
    )(front)
    factors, upper = pl.pallas_call(
        factor_kernel,
        out_shape=[jax.ShapeDtypeStruct((5, W, W), BF16),
                   jax.ShapeDtypeStruct((2 * W, ROWS), BF16)],
        in_specs=[smem, smem, any_space, vmem, any_space],
        out_specs=[vmem, any_space],
        scratch_shapes=[pltpu.VMEM((W, W), F32), pltpu.VMEM((2, W, ROWS), BF16),
                        pltpu.VMEM((2 * W, ROWS), BF16), dma((2,)), dma((NB // 2,))],
        compiler_params=pltpu.CompilerParams(vmem_limit_bytes=60 * MIB),
        name="invert_pivots",
    )(lower_mask, upper_mask, front, corners, strip)
    def group(blocks, slots, depth, tile, rows):
        return [
            pltpu.VMEM(tile + rows + (W,), BF16),
            pltpu.VMEM((blocks, 2, 4, depth, UNIT), BF16),
            pltpu.VMEM((blocks, 2, 2, 4, depth, UNIT), BF16),
            pltpu.VMEM((blocks, 3, 2, 4, depth, UNIT), BF16),
            pltpu.VMEM((slots, 2, depth, UNIT), BF16),
            pltpu.VMEM((blocks, 2, depth, UNIT), BF16),
            pltpu.VMEM((slots, 2, 2, depth, UNIT), F32),
            pltpu.VMEM((blocks, 2, 2, depth, UNIT), F32),
            pltpu.VMEM((slots, 2, 4, depth, UNIT), F32),
            dma(tile), dma((blocks, 2)), dma((blocks, 2, 2)), dma((blocks, 3, 2)),
            dma((slots, 3, 2)), dma((blocks, 3, 2)),
        ]

    main = group(MAIN, 2 * SLOTS, 2 * SHARE, (2, 3, 2), (4, 2, SHARE))
    side = group(SIDE, SIDE, SHARE, (SIDE, 4), (4, SHARE))
    out = pl.pallas_call(
        reduce_kernel,
        out_shape=jax.ShapeDtypeStruct((SHARE, ROWS), F32),
        in_specs=[smem, any_space, any_space, vmem],
        out_specs=vmem,
        scratch_shapes=[
            pltpu.VMEM((2 * W, ROWS), BF16),
            pltpu.VMEM((4, 4, 2, SHARE, 2 * W), BF16),
            pltpu.VMEM((2, 2, SHARE, ROWS), BF16),
            pltpu.VMEM((2 * SLOTS, 2, SHARE, W), F32),
            pltpu.VMEM((2 * SLOTS, SHARE, W), F32),
            pltpu.VMEM((MAIN, SHARE, W), F32),
            pltpu.VMEM((2, 4, 4, SHARE, W), BF16),
            pltpu.VMEM((SIDE, 4, 4, SHARE, W), BF16),
            pltpu.VMEM((SIDE, 4, 4, SHARE, W), BF16),
            dma((1,)), dma((3, 4, 4)), dma((2,)), dma((2 * SLOTS,)), dma((MAIN,)), dma((2,)),
            dma((SIDE,)), dma((SIDE,)),
        ] + main + side,
        compiler_params=pltpu.CompilerParams(collective_id=1, has_side_effects=True,
                                             vmem_limit_bytes=63 * MIB),
        name="reduce_layers",
    )(lower_mask, front.reshape(4, 4, 2, SHARE, ROWS), upper, factors)
    return out.reshape(1, 1, SHARE, ROWS)


def solution(mesh):
    in_specs = (P("rep", "row", "col"), P("rep", None, None), P("rep", None, None))
    out_specs = P("row", "rep", None, "col")
    return jax.shard_map(local, mesh=mesh, in_specs=in_specs, out_specs=out_specs, check_vma=False)
```
